512 devices in a mesh: fsdp: 64 (over y, z_hi, x), tp: 8 (over z_lo, core).
Axes of the slice: x: 4, y: 8, z: 8 (z_hi: 2, z_lo: 4; z = z_hi * 4 + z_lo), core: 2. Of those that a mesh axis runs over, the one named last changes fastest.
Arguments:
- decode_row_inputs: bfloat16 [3, 512, 8192], P(None, 'fsdp'), may hold values from -6 to 6
- lengths: int32 [512], P('fsdp'), may hold values from 2 to 64, as said below
- queries: bfloat16 [3, 512, 8192], P(None, 'fsdp', 'tp'), may hold values from -6 to 6
- rotated_key_cache: bfloat16 [512, 64, 1024], P('fsdp', None, 'tp'), may hold values from -6 to 6
- value_cache_rows: bfloat16 [512, 64, 1024], P('fsdp', None, 'tp'), may hold values from -6 to 6
- key_value_weight: bfloat16 [2, 8192, 1024], P(None, None, 'tp'), may hold values from -0.0625 to 0.0625
- key_value_bias: bfloat16 [2, 1024], P(None, 'tp'), may hold values from -3 to 3
- adapter_down_weight: bfloat16 [8192, 128], P(('fsdp', 'tp')), may hold values from -0.0625 to 0.0625
- adapter_up_weight: bfloat16 [2, 64, 1024], P(None, 'fsdp', 'tp'), may hold values from -0.75 to 0.75
Outputs:
- attended: bfloat16 [3, 512, 8192], P(None, 'fsdp', 'tp')
- new_entries: bfloat16 [2, 3, 512, 1024], P(None, None, 'fsdp', 'tp')
The draws below stay inside these ranges and needn't reach their ends.
Inputs may be any that keep to these rules, and one draw needn't show every extreme that they name: `lengths`: the first row of every aligned block of 8 rows holds 64 cached tokens.
All inputs are finite; a program needn't handle non-finite values.
Results may differ from the reference program's by a relative error of at most 0.0075.
Values may be sent and summed in bfloat16 or wider, within the bound.
A program may use at most 64 MiB of HBM per device.

```python
import jax
import jax.numpy as jnp

MODEL_WIDTH = 8192
HEADS = 64
KEY_VALUE_HEADS = 8
HEAD_SIZE = 128
ADAPTER_RANK = 64
STEPS = 3
ROW_DEV = 8
CACHE = 64
ROWS = 512


def draw_queries(key, part):
    key = jax.random.fold_in(key, 11)
    group = HEADS // KEY_VALUE_HEADS
    shape = (STEPS, ROWS, KEY_VALUE_HEADS, group, HEAD_SIZE)
    result = jax.random.truncated_normal(key, -6.0, 6.0, shape, jnp.float32)
    return result.reshape(STEPS, ROWS, HEADS * HEAD_SIZE).astype(jnp.bfloat16)


def draw_rotated_key_cache(key, part):
    key = jax.random.fold_in(key, 23)
    shape = (ROWS, CACHE, KEY_VALUE_HEADS, HEAD_SIZE)
    result = jax.random.truncated_normal(key, -6.0, 6.0, shape, jnp.float32)
    return result.reshape(ROWS, CACHE, KEY_VALUE_HEADS * HEAD_SIZE).astype(jnp.bfloat16)


def draw_lengths(key, part):
    key = jax.random.fold_in(key, 37)
    drawn = jax.random.randint(key, (ROWS,), 2, CACHE + 1)
    leading = jnp.arange(ROWS, dtype=jnp.int32) % ROW_DEV == 0
    return jnp.where(leading, CACHE, drawn).astype(jnp.int32)


def block_scale(stream_key, shape, cuts, low, top_value):
    def one(dim, blocks):
        steps = jax.random.uniform(jax.random.fold_in(jax.random.fold_in(stream_key, 6), dim), (blocks,), jnp.float32, low / len(cuts), top_value / len(cuts))
        return jnp.repeat(jnp.exp(steps), shape[dim] // blocks).reshape((-1,) + (1,) * (len(shape) - dim - 1))

    loudness = one(*cuts[0])
    for cut in cuts[1:]:
        loudness = loudness * one(*cut)
    return loudness


def scatter_about(key, dims, deviation, limit, cuts=(), kind=jnp.bfloat16):
    values = deviation * jax.random.normal(key, dims, jnp.float32)
    if cuts:
        values = values * block_scale(key, dims, cuts, -0.22, 0.18)
    return jnp.clip(values, -limit, limit).astype(kind)


def setup_inputs(seed: int = 0) -> dict:
    keys = jax.random.split(jax.random.key(seed), 10)
    return {
        "decode_row_inputs": scatter_about(keys[0], (STEPS, ROWS, MODEL_WIDTH), 1.0, 6.0, ((1, 64),)),
        "lengths": draw_lengths(jax.random.fold_in(keys[9], 71), 0),
        "queries": draw_queries(jax.random.fold_in(keys[9], 71), 0),
        "rotated_key_cache": draw_rotated_key_cache(jax.random.fold_in(keys[9], 71), 0),
        "value_cache_rows": scatter_about(keys[4], (ROWS, CACHE, KEY_VALUE_HEADS * HEAD_SIZE), 1.0, 6.0, ((0, 64), (2, 8))),
        "key_value_weight": scatter_about(keys[5], (2, MODEL_WIDTH, KEY_VALUE_HEADS * HEAD_SIZE), MODEL_WIDTH ** -0.5, 0.0625, ((2, 8),)),
        "key_value_bias": scatter_about(keys[6], (2, KEY_VALUE_HEADS * HEAD_SIZE), 0.5, 3.0, ((1, 8),)),
        "adapter_down_weight": scatter_about(keys[7], (MODEL_WIDTH, 2 * ADAPTER_RANK), MODEL_WIDTH ** -0.5, 0.0625, ((0, 512),)),
        "adapter_up_weight": scatter_about(keys[8], (2, ADAPTER_RANK, KEY_VALUE_HEADS * HEAD_SIZE), ADAPTER_RANK ** -0.5, 0.75, ((1, 64), (2, 8))),
    }


ADAPTER_SCALE = 2.0
ROPE_BASE = 1000000.0
MASKED = -1.0e30


def rotary(vectors, positions):
    half_size = vectors.shape[-1] // 2
    frequency = ROPE_BASE ** (-2.0 * jnp.arange(half_size, dtype=jnp.float32) / vectors.shape[-1])
    angle = positions[..., None] * frequency
    cosine = jnp.cos(angle)
    sine = jnp.sin(angle)
    lower = vectors[..., :half_size]
    upper = vectors[..., half_size:]
    return jnp.concatenate([lower * cosine - upper * sine, upper * cosine + lower * sine], axis=-1)


def reference(decode_row_inputs, lengths, queries, rotated_key_cache, value_cache_rows, key_value_weight, key_value_bias, adapter_down_weight, adapter_up_weight):
    key_weight_change = jnp.dot(adapter_down_weight[:, :ADAPTER_RANK], adapter_up_weight[0], preferred_element_type=jnp.float32)
    value_weight_change = jnp.dot(adapter_down_weight[:, ADAPTER_RANK:], adapter_up_weight[1], preferred_element_type=jnp.float32)
    weight_update = jnp.stack([key_weight_change, value_weight_change])
    merged_weight = (key_value_weight.astype(jnp.float32) + ADAPTER_SCALE * weight_update).astype(jnp.bfloat16)
    flattened = decode_row_inputs.reshape(STEPS * ROWS, MODEL_WIDTH)
    key_part = jnp.dot(flattened, merged_weight[0], preferred_element_type=jnp.float32) + key_value_bias[0].astype(jnp.float32)
    value_part = jnp.dot(flattened, merged_weight[1], preferred_element_type=jnp.float32) + key_value_bias[1].astype(jnp.float32)
    positions = (lengths[None, :] + jnp.arange(STEPS, dtype=jnp.int32)[:, None]).astype(jnp.float32)
    fresh_keys = rotary(key_part.reshape(STEPS, ROWS, KEY_VALUE_HEADS, HEAD_SIZE), positions[:, :, None]).astype(jnp.bfloat16)
    fresh_values = value_part.reshape(STEPS, ROWS, KEY_VALUE_HEADS, HEAD_SIZE).astype(jnp.bfloat16)
    group = HEADS // KEY_VALUE_HEADS
    scale_factor = HEAD_SIZE ** -0.5
    grouped_queries = queries.reshape(STEPS, ROWS, KEY_VALUE_HEADS, group, HEAD_SIZE).astype(jnp.float32)
    stored_keys = rotated_key_cache.reshape(ROWS, CACHE, KEY_VALUE_HEADS, HEAD_SIZE).astype(jnp.float32)
    stored_values = value_cache_rows.reshape(ROWS, CACHE, KEY_VALUE_HEADS, HEAD_SIZE).astype(jnp.float32)
    cached_scores = jnp.einsum("sbkgd,blkd->sbkgl", grouped_queries, stored_keys) * scale_factor
    valid = jnp.arange(CACHE, dtype=jnp.int32)[None, :] < lengths[:, None]
    cached_scores = jnp.where(valid[None, :, None, None, :], cached_scores, MASKED)
    fresh_scores = jnp.einsum("sbkgd,tbkd->sbkgt", grouped_queries, fresh_keys.astype(jnp.float32)) * scale_factor
    causal = jnp.arange(STEPS, dtype=jnp.int32)[None, :] <= jnp.arange(STEPS, dtype=jnp.int32)[:, None]
    fresh_scores = jnp.where(causal[:, None, None, None, :], fresh_scores, MASKED)
    scores = jnp.concatenate([cached_scores, fresh_scores], axis=-1)
    peak = jnp.max(scores, axis=-1, keepdims=True)
    raised = jnp.exp(scores - peak)
    weights = (raised / jnp.sum(raised, axis=-1, keepdims=True)).astype(jnp.bfloat16)
    attended = jnp.einsum("sbkgl,blkd->sbkgd", weights[..., :CACHE].astype(jnp.float32), stored_values)
    attended = attended + jnp.einsum("sbkgt,tbkd->sbkgd", weights[..., CACHE:].astype(jnp.float32), fresh_values.astype(jnp.float32))
    attended = attended.astype(jnp.bfloat16).reshape(STEPS, ROWS, HEADS * HEAD_SIZE)
    entries = jnp.stack([fresh_keys.reshape(STEPS, ROWS, KEY_VALUE_HEADS * HEAD_SIZE), fresh_values.reshape(STEPS, ROWS, KEY_VALUE_HEADS * HEAD_SIZE)])
    return attended, entries
```

```python
import functools
import math

import jax
import jax.numpy as jnp
from jax import lax
from jax.experimental import pallas as pl
from jax.experimental.pallas import tpu as pltpu
from jax.sharding import PartitionSpec as P

HEAD = 128
GROUP = 8
STEPS = 3
ROWS = 8
CACHE = 64
NX = 4
ADAPTER_SCALE = 2.0
ROPE_BASE = 1000000.0
MASKED = -1e30
MESH = pl.DeviceIdType.MESH
F32 = jnp.float32
BF16 = jnp.bfloat16
N = STEPS * ROWS
M = STEPS * GROUP * ROWS
SLOTS = ROWS * CACHE
W_PARTS = 8


def iota(shape, dim):
    return lax.broadcasted_iota(jnp.int32, shape, dim)


def dot(a, b):
    return jnp.dot(a, b, preferred_element_type=F32)


def dot_t(a, b):
    return lax.dot_general(a, b, (((1,), (1,)), ((), ())), preferred_element_type=F32)


def stack_steps(ref, columns):
    return jnp.concatenate([ref[s, :, columns].astype(F32) for s in range(STEPS)], axis=0)


def kernel(
    nq,
    ntp,
    x_hbm,
    len_hbm,
    q_hbm,
    k_hbm,
    v_hbm,
    w_hbm,
    bias_hbm,
    d_hbm,
    u_hbm,
    att_hbm,
    ent_hbm,
    x_v,
    len_s,
    q_v,
    k_v,
    v_v,
    w_v,
    bias_v,
    u_v,
    d_all,
    xs,
    xr,
    u1,
    u2,
    pp,
    pr,
    pt,
    xb,
    proj,
    cos_v,
    sin_v,
    qb,
    peak_c,
    total_c,
    acc_c,
    ublk,
    att_v,
    ent_v,
    in_sem,
    w_sem,
    out_sem,
    d_send,
    d_recv,
    x_send,
    x_recv,
    u1_send,
    u1_recv,
    u2_send,
    u2_recv,
    p_send,
    p_recv,
    t_send,
    t_recv,
):
    f = lax.axis_index("fsdp")
    t = lax.axis_index("tp")
    q = f // NX
    x = lax.rem(f, NX)
    d_rows = d_all.shape[1]
    width = x_v.shape[2]

    loads = {}
    for i, (name, src, dst) in enumerate(
        [
            ("d", d_hbm, d_all.at[q]),
            ("u", u_hbm, u_v),
            ("x", x_hbm, x_v),
            ("len", len_hbm, len_s),
            ("bias", bias_hbm, bias_v),
            ("q", q_hbm, q_v),
            ("k", k_hbm, k_v),
            ("v", v_hbm, v_v),
        ]
    ):
        loads[name] = pltpu.make_async_copy(src, dst, in_sem.at[i])
        loads[name].start()
    part = width // W_PARTS

    def w_load(i):
        rows = pl.ds(pl.multiple_of(i * part, part), part)
        return pltpu.make_async_copy(w_hbm.at[:, rows], w_v.at[:, rows], w_sem.at[i])

    for i in range(W_PARTS):
        w_load(i).start()

    def at_q(d):
        return lax.rem(q + d, nq) * NX + x

    def at_x(d):
        return q * NX + lax.rem(x + d, NX)

    def at_t(d):
        return lax.rem(t + d, ntp)

    barrier = pltpu.get_barrier_semaphore()
    for d in range(1, nq):
        pl.semaphore_signal(barrier, inc=1, device_id=(at_q(d), t), device_id_type=MESH)
    for d in range(1, NX):
        pl.semaphore_signal(barrier, inc=1, device_id=(at_x(d), t), device_id_type=MESH)
    for d in range(1, ntp):
        pl.semaphore_signal(barrier, inc=1, device_id=(f, at_t(d)), device_id_type=MESH)

    loads["u"].wait()
    u1[q] = jnp.concatenate([u_v[0], u_v[1]], axis=1).astype(F32)
    span = ntp * d_rows
    per = HEAD // d_rows
    groups = nq // per
    pick = (
        lax.rem(iota((per * span, HEAD), 0), span)
        == t * d_rows + lax.rem(iota((per * span, HEAD), 1), d_rows)
    ) & (iota((per * span, HEAD), 0) // span == iota((per * span, HEAD), 1) // d_rows)
    pick = jnp.where(pick, 1.0, 0.0).astype(BF16)
    loads["x"].wait()
    rows = []
    for j in range(NX):
        for g in range(groups):
            rows.append(
                jnp.concatenate(
                    [
                        stack_steps(x_v, pl.ds(((g * per + i) * NX + j) * span, span))
                        for i in range(per)
                    ],
                    axis=1,
                )
            )
    picked = dot(jnp.concatenate(rows, axis=0).astype(BF16), pick)
    for j in range(NX):
        for g in range(groups):
            base = (j * groups + g) * N
            for s in range(STEPS):
                xs[j, s, :, g * HEAD : (g + 1) * HEAD] = picked[
                    base + s * ROWS : base + (s + 1) * ROWS
                ].astype(BF16)
    xr[x] = xs[x]
    loads["d"].wait()

    pl.semaphore_wait(barrier, nq - 1 + NX - 1 + ntp - 1)

    def remote(src, dst, send, recv, where):
        return pltpu.make_async_remote_copy(
            src_ref=src, dst_ref=dst, send_sem=send, recv_sem=recv, device_id=where, device_id_type=MESH
        )

    def from_q(d):
        return lax.rem(q + nq - d, nq)

    def from_x(d):
        return lax.rem(x + NX - d, NX)

    def from_t(d):
        return lax.rem(t + ntp - d, ntp)

    def d_copy(d, block):
        return remote(d_all.at[block], d_all.at[block], d_send.at[d], d_recv.at[d], (at_q(d), t))

    def u1_copy(d, block):
        return remote(u1.at[block], u1.at[block], u1_send.at[d], u1_recv.at[d], (at_q(d), t))

    def x_copy(d, block):
        return remote(xs.at[lax.rem(x + d, NX)], xr.at[block], x_send.at[d], x_recv.at[d], (at_x(d), t))

    def u2_copy(d, block):
        return remote(u2.at[block], u2.at[block], u2_send.at[d], u2_recv.at[d], (at_x(d), t))

    def p_copy(d, block):
        return remote(pp.at[lax.rem(x + d, NX)], pr.at[block], p_send.at[d], p_recv.at[d], (at_x(d), t))

    def t_copy(d, block):
        return remote(pt.at[block], pt.at[block], t_send.at[d], t_recv.at[d], (f, at_t(d)))

    for d in range(1, NX):
        x_copy(d, x).start()
    for d in range(1, nq):
        d_copy(d, q).start()
    for d in range(1, nq):
        u1_copy(d, q).start()

    for name in ("q", "k", "len"):
        loads[name].wait()
    queries = jnp.concatenate(
        [
            q_v[s, :, h * HEAD : (h + 1) * HEAD].astype(F32)
            for s in range(STEPS)
            for h in range(GROUP)
        ],
        axis=0,
    ).astype(BF16)
    qb[...] = queries
    scale = HEAD**-0.5
    row = iota((ROWS, HEAD), 0)
    length = jnp.zeros((ROWS, HEAD), jnp.int32)
    for b in range(ROWS):
        length = jnp.where(row == b, len_s[b], length)
    column = iota((ROWS, SLOTS), 1)
    valid = (column // CACHE == iota((ROWS, SLOTS), 0)) & (
        lax.rem(column, CACHE) < jnp.concatenate([length] * (SLOTS // HEAD), axis=1)
    )
    scores = dot_t(queries, k_v[...].reshape(SLOTS, HEAD)) * scale
    scores = jnp.where(
        valid[None], scores.reshape(STEPS * GROUP, ROWS, SLOTS), MASKED
    ).reshape(M, SLOTS)
    peak = jnp.max(scores, axis=-1, keepdims=True)
    raised = jnp.exp(scores - peak)
    peak_c[...] = jnp.broadcast_to(peak, (M, HEAD))
    total_c[...] = jnp.broadcast_to(jnp.sum(raised, axis=-1, keepdims=True), (M, HEAD))
    loads["v"].wait()
    acc_c[...] = dot(raised.astype(BF16), v_v[...].reshape(SLOTS, HEAD))

    for d in range(1, NX):
        x_copy(d, from_x(d)).wait_recv()
    for d in range(1, nq):
        d_copy(d, from_q(d)).wait_recv()
    mine = jnp.concatenate([stack_steps(xr.at[j], slice(None)) for j in range(NX)], axis=0)
    partial = dot(mine.astype(BF16), d_all[...].reshape(nq * d_rows, HEAD))
    for j in range(NX):
        for s in range(STEPS):
            base = j * N + s * ROWS
            pp[j, s] = partial[base : base + ROWS]
    for d in range(1, NX):
        p_copy(d, x).start()
    pr[x] = pp[x]
    for d in range(1, nq):
        u1_copy(d, from_q(d)).wait_recv()
    u2[x] = u1[...].reshape(nq, 2 * HEAD).astype(BF16)
    for d in range(1, NX):
        u2_copy(d, x).start()

    for s in range(STEPS):
        xb[pl.ds(s * ROWS, ROWS)] = x_v[s].astype(F32)
    proj[...] = jnp.zeros_like(proj)

    def project(i, carry):
        w_load(i).wait()
        rows = pl.ds(pl.multiple_of(i * part, part), part)
        proj[...] += dot(
            xb[:, rows].astype(BF16), jnp.concatenate([w_v[0, rows], w_v[1, rows]], axis=1)
        )
        return carry

    lax.fori_loop(0, W_PARTS // 2, project, 0)

    loads["bias"].wait()
    half = HEAD // 2
    lane = iota((ROWS, HEAD), 1)
    frequency = jnp.exp(lax.rem(lane, half).astype(F32) * (-2.0 / HEAD * math.log(ROPE_BASE)))
    for s in range(STEPS):
        angle = (length + s).astype(F32) * frequency
        cos_v[pl.ds(s * ROWS, ROWS)] = jnp.cos(angle)
        sine = jnp.sin(angle)
        sin_v[pl.ds(s * ROWS, ROWS)] = jnp.where(lane < half, -sine, sine)

    for d in range(1, NX):
        p_copy(d, from_x(d)).wait_recv()
    for s in range(STEPS):
        pt[t, s] = pr[0, s] + pr[1, s] + pr[2, s] + pr[3, s]
    for d in range(1, ntp):
        t_copy(d, t).start()

    lax.fori_loop(W_PARTS // 2, W_PARTS, project, 0)
    bias = jnp.concatenate([bias_v[0:1], bias_v[1:2]], axis=1).astype(F32)
    proj[...] += bias
    for d in range(1, NX):
        u2_copy(d, from_x(d)).wait_recv()
    ranks = nq * NX
    order = iota((ranks, ranks), 0)
    order = iota((ranks, ranks), 1) == lax.rem(order, NX) * nq + order // NX
    up = dot(jnp.where(order, 1.0, 0.0).astype(BF16), u2[...].reshape(ranks, 2 * HEAD))
    up = up * ADAPTER_SCALE
    which = iota((ranks, 2 * HEAD), 1) < HEAD
    ublk[...] = jnp.concatenate(
        [jnp.where(which, up, 0.0), jnp.where(which, 0.0, up)], axis=0
    ).astype(BF16)

    for d in range(1, ntp):
        t_copy(d, from_t(d)).wait_recv()
    sums = []
    for s in range(STEPS):
        total = pt[0, s]
        for i in range(1, ntp):
            total = total + pt[i, s]
        sums.append(total)
    low_rank = jnp.concatenate(sums, axis=0)
    high = low_rank.astype(BF16).astype(F32)
    both = jnp.concatenate([high, low_rank - high], axis=0).astype(BF16)
    change = dot(both, ublk[...])
    fresh = proj[...] + change[:N] + change[N:]
    key = fresh[:, :HEAD]
    key = key * cos_v[...] + pltpu.roll(key, half, axis=1) * sin_v[...]
    value = fresh[:, HEAD:]
    for s in range(STEPS):
        ent_v[0, s] = key[s * ROWS : (s + 1) * ROWS].astype(BF16)
        ent_v[1, s] = value[s * ROWS : (s + 1) * ROWS].astype(BF16)
    ent_out = pltpu.make_async_copy(ent_v, ent_hbm, out_sem.at[0])
    ent_out.start()
    scores = dot_t(qb[...], key.astype(BF16)) * scale
    r, c = iota((M, N), 0), iota((M, N), 1)
    scores = jnp.where(
        (lax.rem(r, ROWS) == lax.rem(c, ROWS)) & (c // ROWS <= r // (GROUP * ROWS)), scores, MASKED
    )
    peak_old = peak_c[:, 0:1]
    peak = jnp.maximum(peak_old, jnp.max(scores, axis=-1, keepdims=True))
    raised = jnp.exp(scores - peak)
    shrink = jnp.exp(peak_old - peak)
    total = shrink * total_c[:, 0:1] + jnp.sum(raised, axis=-1, keepdims=True)
    out = (shrink * acc_c[...] + dot(raised.astype(BF16), value.astype(BF16))) / total
    for s in range(STEPS):
        for h in range(GROUP):
            base = (s * GROUP + h) * ROWS
            att_v[s, :, h * HEAD : (h + 1) * HEAD] = out[base : base + ROWS].astype(BF16)
    att_out = pltpu.make_async_copy(att_v, att_hbm, out_sem.at[1])
    att_out.start()

    for d in range(1, NX):
        x_copy(d, x).wait_send()
        p_copy(d, x).wait_send()
        u2_copy(d, x).wait_send()
    for d in range(1, nq):
        d_copy(d, q).wait_send()
        u1_copy(d, q).wait_send()
    for d in range(1, ntp):
        t_copy(d, t).wait_send()
    ent_out.wait()
    att_out.wait()


def body(ntp, x, lengths, queries, keys, values, weight, bias, down, up):
    width = x.shape[2]
    d_rows = down.shape[0]
    nq = width // (ntp * d_rows) // NX
    vmem = pltpu.VMEM
    dma = pltpu.SemaphoreType.DMA
    return pl.pallas_call(
        functools.partial(kernel, nq, ntp),
        out_shape=(
            jax.ShapeDtypeStruct(queries.shape, BF16),
            jax.ShapeDtypeStruct((2, STEPS, ROWS, HEAD), BF16),
        ),
        in_specs=[pl.BlockSpec(memory_space=pl.ANY)] * 9,
        out_specs=(pl.BlockSpec(memory_space=pl.ANY),) * 2,
        scratch_shapes=[
            vmem(x.shape, BF16),
            pltpu.SMEM(lengths.shape, jnp.int32),
            vmem(queries.shape, BF16),
            vmem(keys.shape, BF16),
            vmem(values.shape, BF16),
            vmem(weight.shape, BF16),
            vmem(bias.shape, BF16),
            vmem(up.shape, BF16),
            vmem((nq, d_rows, HEAD), BF16),
            vmem((NX, STEPS, ROWS, nq * d_rows), BF16),
            vmem((NX, STEPS, ROWS, nq * d_rows), BF16),
            vmem((nq, 1, 2 * HEAD), F32),
            vmem((NX, nq, 2 * HEAD), BF16),
            vmem((NX, STEPS, ROWS, HEAD), F32),
            vmem((NX, STEPS, ROWS, HEAD), F32),
            vmem((ntp, STEPS, ROWS, HEAD), F32),
            vmem((N, width), F32),
            vmem((N, 2 * HEAD), F32),
            vmem((N, HEAD), F32),
            vmem((N, HEAD), F32),
            vmem((M, HEAD), BF16),
            vmem((M, HEAD), F32),
            vmem((M, HEAD), F32),
            vmem((M, HEAD), F32),
            vmem((2 * nq * NX, 2 * HEAD), BF16),
            vmem(queries.shape, BF16),
            vmem((2, STEPS, ROWS, HEAD), BF16),
            dma((8,)),
            dma((W_PARTS,)),
            dma((2,)),
            dma((nq,)),
            dma((nq,)),
            dma((NX,)),
            dma((NX,)),
            dma((nq,)),
            dma((nq,)),
            dma((NX,)),
            dma((NX,)),
            dma((NX,)),
            dma((NX,)),
            dma((ntp,)),
            dma((ntp,)),
        ],
        compiler_params=pltpu.CompilerParams(
            collective_id=0, has_side_effects=True, vmem_limit_bytes=48 * 1024 * 1024
        ),
        name="adapter_attention",
    )(x, lengths, queries, keys, values, weight, bias, down, up)


def solution(mesh):
    placed = (
        P(None, "fsdp", None),
        P("fsdp"),
        P(None, "fsdp", "tp"),
        P("fsdp", None, "tp"),
        P("fsdp", None, "tp"),
        P(None, None, "tp"),
        P(None, "tp"),
        P(("fsdp", "tp"), None),
        P(None, "fsdp", "tp"),
    )
    return jax.shard_map(
        functools.partial(body, mesh.shape["tp"]),
        mesh=mesh,
        in_specs=placed,
        out_specs=(P(None, "fsdp", "tp"), P(None, None, "fsdp", "tp")),
        check_vma=False,
    )
```

```python
import functools
import math

import jax
import jax.numpy as jnp
from jax import lax
from jax.experimental import pallas as pl
from jax.experimental.pallas import tpu as pltpu
from jax.sharding import PartitionSpec as P

HEAD = 128
GROUP = 8
STEPS = 3
ROWS = 8
CACHE = 64
NX = 4
ADAPTER_SCALE = 2.0
ROPE_BASE = 1000000.0
MASKED = -1e30
MESH = pl.DeviceIdType.MESH
F32 = jnp.float32
BF16 = jnp.bfloat16
N = STEPS * ROWS
M = STEPS * GROUP * ROWS
SLOTS = ROWS * CACHE
W_PARTS = 8


def iota(shape, dim):
    return lax.broadcasted_iota(jnp.int32, shape, dim)


def dot(a, b):
    return jnp.dot(a, b, preferred_element_type=F32)


def dot_t(a, b):
    return lax.dot_general(a, b, (((1,), (1,)), ((), ())), preferred_element_type=F32)


def stack_steps(ref, columns):
    return jnp.concatenate([ref[s, :, columns].astype(F32) for s in range(STEPS)], axis=0)


def kernel(
    nq,
    ntp,
    x_hbm,
    len_hbm,
    q_hbm,
    k_hbm,
    v_hbm,
    w_hbm,
    bias_hbm,
    d_hbm,
    u_hbm,
    att_v,
    ent_v,
    x_v,
    len_s,
    q_v,
    k_v,
    v_v,
    w_v,
    bias_v,
    u_v,
    d_all,
    xs,
    xr,
    u1,
    u2,
    pp,
    pr,
    pt,
    xb,
    proj,
    cos_v,
    sin_v,
    qb,
    peak_c,
    total_c,
    acc_c,
    ublk,
    in_sem,
    w_sem,
    d_send,
    d_recv,
    x_send,
    x_recv,
    u1_send,
    u1_recv,
    u2_send,
    u2_recv,
    p_send,
    p_recv,
    t_send,
    t_recv,
):
    f = lax.axis_index("fsdp")
    t = lax.axis_index("tp")
    q = f // NX
    x = lax.rem(f, NX)
    d_rows = d_all.shape[1]
    width = x_v.shape[2]

    loads = {}
    for i, (name, src, dst) in enumerate(
        [
            ("d", d_hbm, d_all.at[q]),
            ("u", u_hbm, u_v),
            ("x", x_hbm, x_v),
            ("len", len_hbm, len_s),
            ("bias", bias_hbm, bias_v),
            ("q", q_hbm, q_v),
            ("k", k_hbm, k_v),
            ("v", v_hbm, v_v),
        ]
    ):
        loads[name] = pltpu.make_async_copy(src, dst, in_sem.at[i])
        loads[name].start()
    part = width // W_PARTS

    def w_load(i):
        rows = pl.ds(pl.multiple_of(i * part, part), part)
        return pltpu.make_async_copy(w_hbm.at[:, rows], w_v.at[:, rows], w_sem.at[i])

    for i in range(W_PARTS):
        w_load(i).start()

    def at_q(d):
        return lax.rem(q + d, nq) * NX + x

    def at_x(d):
        return q * NX + lax.rem(x + d, NX)

    def at_t(d):
        return lax.rem(t + d, ntp)

    barrier = pltpu.get_barrier_semaphore()
    for d in range(1, nq):
        pl.semaphore_signal(barrier, inc=1, device_id=(at_q(d), t), device_id_type=MESH)
    for d in range(1, NX):
        pl.semaphore_signal(barrier, inc=1, device_id=(at_x(d), t), device_id_type=MESH)
    for d in range(1, ntp):
        pl.semaphore_signal(barrier, inc=1, device_id=(f, at_t(d)), device_id_type=MESH)

    loads["u"].wait()
    u1[q] = jnp.concatenate([u_v[0:1].astype(F32), u_v[1:2].astype(F32)], axis=1)
    span = ntp * d_rows
    per = HEAD // d_rows
    groups = nq // per
    pick = (
        lax.rem(iota((per * span, HEAD), 0), span)
        == t * d_rows + lax.rem(iota((per * span, HEAD), 1), d_rows)
    ) & (iota((per * span, HEAD), 0) // span == iota((per * span, HEAD), 1) // d_rows)
    pick = jnp.where(pick, 1.0, 0.0).astype(BF16)
    loads["x"].wait()
    rows = []
    for j in range(NX):
        for g in range(groups):
            rows.append(
                jnp.concatenate(
                    [
                        stack_steps(x_v, pl.ds(((g * per + i) * NX + j) * span, span))
                        for i in range(per)
                    ],
                    axis=1,
                )
            )
    picked = dot(jnp.concatenate(rows, axis=0).astype(BF16), pick)
    for j in range(NX):
        for g in range(groups):
            base = (j * groups + g) * N
            for s in range(STEPS):
                xs[j, s, :, g * HEAD : (g + 1) * HEAD] = picked[
                    base + s * ROWS : base + (s + 1) * ROWS
                ].astype(BF16)
    xr[x] = xs[x]
    loads["d"].wait()

    pl.semaphore_wait(barrier, nq - 1 + NX - 1 + ntp - 1)

    def remote(src, dst, send, recv, where):
        return pltpu.make_async_remote_copy(
            src_ref=src, dst_ref=dst, send_sem=send, recv_sem=recv, device_id=where, device_id_type=MESH
        )

    def from_q(d):
        return lax.rem(q + nq - d, nq)

    def from_x(d):
        return lax.rem(x + NX - d, NX)

    def from_t(d):
        return lax.rem(t + ntp - d, ntp)

    def d_copy(d, block):
        return remote(d_all.at[block], d_all.at[block], d_send.at[d], d_recv.at[d], (at_q(d), t))

    def u1_copy(d, block):
        return remote(u1.at[block], u1.at[block], u1_send.at[d], u1_recv.at[d], (at_q(d), t))

    def x_copy(d, block):
        return remote(xs.at[lax.rem(x + d, NX)], xr.at[block], x_send.at[d], x_recv.at[d], (at_x(d), t))

    def u2_copy(d, block):
        return remote(u2.at[block], u2.at[block], u2_send.at[d], u2_recv.at[d], (at_x(d), t))

    def p_copy(d, block):
        return remote(pp.at[lax.rem(x + d, NX)], pr.at[block], p_send.at[d], p_recv.at[d], (at_x(d), t))

    def t_copy(d, block):
        return remote(pt.at[block], pt.at[block], t_send.at[d], t_recv.at[d], (f, at_t(d)))

    for d in range(1, NX):
        x_copy(d, x).start()
    for d in range(1, nq):
        d_copy(d, q).start()
    for d in range(1, nq):
        u1_copy(d, q).start()

    for name in ("q", "k", "len"):
        loads[name].wait()
    queries = jnp.concatenate(
        [
            q_v[s, :, h * HEAD : (h + 1) * HEAD].astype(F32)
            for s in range(STEPS)
            for h in range(GROUP)
        ],
        axis=0,
    ).astype(BF16)
    qb[...] = queries
    scale = HEAD**-0.5
    row = iota((ROWS, HEAD), 0)
    length = jnp.zeros((ROWS, HEAD), jnp.int32)
    for b in range(ROWS):
        length = jnp.where(row == b, len_s[b], length)
    column = iota((ROWS, SLOTS), 1)
    valid = (column // CACHE == iota((ROWS, SLOTS), 0)) & (
        lax.rem(column, CACHE) < jnp.concatenate([length] * (SLOTS // HEAD), axis=1)
    )
    scores = dot_t(queries, k_v[...].reshape(SLOTS, HEAD)) * scale
    scores = jnp.where(
        valid[None], scores.reshape(STEPS * GROUP, ROWS, SLOTS), MASKED
    ).reshape(M, SLOTS)
    peak = jnp.max(scores, axis=-1, keepdims=True)
    raised = jnp.exp(scores - peak)
    peak_c[...] = jnp.broadcast_to(peak, (M, HEAD))
    total_c[...] = jnp.broadcast_to(jnp.sum(raised, axis=-1, keepdims=True), (M, HEAD))
    loads["v"].wait()
    acc_c[...] = dot(raised.astype(BF16), v_v[...].reshape(SLOTS, HEAD))

    for d in range(1, NX):
        x_copy(d, from_x(d)).wait_recv()
    for d in range(1, nq):
        d_copy(d, from_q(d)).wait_recv()
    mine = jnp.concatenate([stack_steps(xr.at[j], slice(None)) for j in range(NX)], axis=0)
    partial = dot(mine.astype(BF16), d_all[...].reshape(nq * d_rows, HEAD))
    for j in range(NX):
        for s in range(STEPS):
            base = j * N + s * ROWS
            pp[j, s] = partial[base : base + ROWS]
    for d in range(1, NX):
        p_copy(d, x).start()
    pr[x] = pp[x]
    for d in range(1, nq):
        u1_copy(d, from_q(d)).wait_recv()
    u2[x] = u1[...].reshape(nq, 2 * HEAD).astype(BF16)
    for d in range(1, NX):
        u2_copy(d, x).start()

    for s in range(STEPS):
        xb[pl.ds(s * ROWS, ROWS)] = x_v[s].astype(F32)
    proj[...] = jnp.zeros_like(proj)

    def project(i, carry):
        w_load(i).wait()
        rows = pl.ds(pl.multiple_of(i * part, part), part)
        proj[...] += dot(
            xb[:, rows].astype(BF16), jnp.concatenate([w_v[0, rows], w_v[1, rows]], axis=1)
        )
        return carry

    lax.fori_loop(0, W_PARTS // 2, project, 0)

    loads["bias"].wait()
    half = HEAD // 2
    lane = iota((ROWS, HEAD), 1)
    frequency = jnp.exp(lax.rem(lane, half).astype(F32) * (-2.0 / HEAD * math.log(ROPE_BASE)))
    for s in range(STEPS):
        angle = (length + s).astype(F32) * frequency
        cos_v[pl.ds(s * ROWS, ROWS)] = jnp.cos(angle)
        sine = jnp.sin(angle)
        sin_v[pl.ds(s * ROWS, ROWS)] = jnp.where(lane < half, -sine, sine)

    for d in range(1, NX):
        p_copy(d, from_x(d)).wait_recv()
    for s in range(STEPS):
        pt[t, s] = pr[0, s] + pr[1, s] + pr[2, s] + pr[3, s]
    for d in range(1, ntp):
        t_copy(d, t).start()

    lax.fori_loop(W_PARTS // 2, W_PARTS, project, 0)
    bias = jnp.concatenate([bias_v[0:1], bias_v[1:2]], axis=1).astype(F32)
    proj[...] += bias
    for d in range(1, NX):
        u2_copy(d, from_x(d)).wait_recv()
    ranks = nq * NX
    order = iota((ranks, ranks), 0)
    order = iota((ranks, ranks), 1) == lax.rem(order, NX) * nq + order // NX
    up = dot(jnp.where(order, 1.0, 0.0).astype(BF16), u2[...].reshape(ranks, 2 * HEAD))
    up = up * ADAPTER_SCALE
    which = iota((ranks, 2 * HEAD), 1) < HEAD
    ublk[...] = jnp.concatenate(
        [jnp.where(which, up, 0.0), jnp.where(which, 0.0, up)], axis=0
    ).astype(BF16)

    for d in range(1, ntp):
        t_copy(d, from_t(d)).wait_recv()
    sums = []
    for s in range(STEPS):
        total = pt[0, s]
        for i in range(1, ntp):
            total = total + pt[i, s]
        sums.append(total)
    low_rank = jnp.concatenate(sums, axis=0)
    high = low_rank.astype(BF16).astype(F32)
    both = jnp.concatenate([high, low_rank - high], axis=0).astype(BF16)
    change = dot(both, ublk[...])
    fresh = proj[...] + change[:N] + change[N:]
    key = fresh[:, :HEAD]
    key = key * cos_v[...] + pltpu.roll(key, half, axis=1) * sin_v[...]
    value = fresh[:, HEAD:]
    for s in range(STEPS):
        ent_v[0, s] = key[s * ROWS : (s + 1) * ROWS].astype(BF16)
        ent_v[1, s] = value[s * ROWS : (s + 1) * ROWS].astype(BF16)
    scores = dot_t(qb[...], key.astype(BF16)) * scale
    r, c = iota((M, N), 0), iota((M, N), 1)
    scores = jnp.where(
        (lax.rem(r, ROWS) == lax.rem(c, ROWS)) & (c // ROWS <= r // (GROUP * ROWS)), scores, MASKED
    )
    peak_old = peak_c[:, 0:1]
    peak = jnp.maximum(peak_old, jnp.max(scores, axis=-1, keepdims=True))
    raised = jnp.exp(scores - peak)
    shrink = jnp.exp(peak_old - peak)
    total = shrink * total_c[:, 0:1] + jnp.sum(raised, axis=-1, keepdims=True)
    out = (shrink * acc_c[...] + dot(raised.astype(BF16), value.astype(BF16))) / total
    for s in range(STEPS):
        for h in range(GROUP):
            base = (s * GROUP + h) * ROWS
            att_v[s, :, h * HEAD : (h + 1) * HEAD] = out[base : base + ROWS].astype(BF16)

    for d in range(1, NX):
        x_copy(d, x).wait_send()
        p_copy(d, x).wait_send()
        u2_copy(d, x).wait_send()
    for d in range(1, nq):
        d_copy(d, q).wait_send()
        u1_copy(d, q).wait_send()
    for d in range(1, ntp):
        t_copy(d, t).wait_send()


def deliver(att_v, ent_v, att_hbm, ent_hbm, sem):
    copies = [
        pltpu.make_async_copy(att_v, att_hbm, sem.at[0]),
        pltpu.make_async_copy(ent_v, ent_hbm, sem.at[1]),
    ]
    for copy in copies:
        copy.start()
    for copy in copies:
        copy.wait()


def body(ntp, x, lengths, queries, keys, values, weight, bias, down, up):
    width = x.shape[2]
    d_rows = down.shape[0]
    nq = width // (ntp * d_rows) // NX
    vmem = pltpu.VMEM
    dma = pltpu.SemaphoreType.DMA
    anywhere = pl.BlockSpec(memory_space=pl.ANY)
    inside = pl.BlockSpec(memory_space=pltpu.VMEM)
    entries = (2, STEPS, ROWS, HEAD)
    attended, entry = pl.pallas_call(
        functools.partial(kernel, nq, ntp),
        out_shape=(pltpu.VMEM(queries.shape, BF16), pltpu.VMEM(entries, BF16)),
        in_specs=[anywhere] * 9,
        out_specs=(inside, inside),
        scratch_shapes=[
            vmem(x.shape, BF16),
            pltpu.SMEM(lengths.shape, jnp.int32),
            vmem(queries.shape, BF16),
            vmem(keys.shape, BF16),
            vmem(values.shape, BF16),
            vmem(weight.shape, BF16),
            vmem(bias.shape, BF16),
            vmem((2, HEAD), BF16),
            vmem((nq, d_rows, HEAD), BF16),
            vmem((NX, STEPS, ROWS, nq * d_rows), BF16),
            vmem((NX, STEPS, ROWS, nq * d_rows), BF16),
            vmem((nq, 1, 2 * HEAD), F32),
            vmem((NX, nq, 2 * HEAD), BF16),
            vmem((NX, STEPS, ROWS, HEAD), F32),
            vmem((NX, STEPS, ROWS, HEAD), F32),
            vmem((ntp, STEPS, ROWS, HEAD), F32),
            vmem((N, width), F32),
            vmem((N, 2 * HEAD), F32),
            vmem((N, HEAD), F32),
            vmem((N, HEAD), F32),
            vmem((M, HEAD), BF16),
            vmem((M, HEAD), F32),
            vmem((M, HEAD), F32),
            vmem((M, HEAD), F32),
            vmem((2 * nq * NX, 2 * HEAD), BF16),
            dma((8,)),
            dma((W_PARTS,)),
            dma((nq,)),
            dma((nq,)),
            dma((NX,)),
            dma((NX,)),
            dma((nq,)),
            dma((nq,)),
            dma((NX,)),
            dma((NX,)),
            dma((NX,)),
            dma((NX,)),
            dma((ntp,)),
            dma((ntp,)),
        ],
        compiler_params=pltpu.CompilerParams(
            collective_id=0, has_side_effects=True, vmem_limit_bytes=60 * 1024 * 1024
        ),
        name="adapter_attention",
    )(x, lengths, queries, keys, values, weight, bias, down, up.reshape(2, HEAD))
    return pl.pallas_call(
        deliver,
        out_shape=(
            jax.ShapeDtypeStruct(queries.shape, BF16),
            jax.ShapeDtypeStruct(entries, BF16),
        ),
        in_specs=[inside] * 2,
        out_specs=(anywhere, anywhere),
        scratch_shapes=[dma((2,))],
        compiler_params=pltpu.CompilerParams(vmem_limit_bytes=1024 * 1024),
        name="deliver",
    )(attended, entry)


def solution(mesh):
    placed = (
        P(None, "fsdp", None),
        P("fsdp"),
        P(None, "fsdp", "tp"),
        P("fsdp", None, "tp"),
        P("fsdp", None, "tp"),
        P(None, None, "tp"),
        P(None, "tp"),
        P(("fsdp", "tp"), None),
        P(None, "fsdp", "tp"),
    )
    return jax.shard_map(
        functools.partial(body, mesh.shape["tp"]),
        mesh=mesh,
        in_specs=placed,
        out_specs=(P(None, "fsdp", "tp"), P(None, None, "fsdp", "tp")),
        check_vma=False,
    )
```

```python
import math

import jax
import jax.numpy as jnp
from jax import lax
from jax.experimental import pallas as pl
from jax.experimental.pallas import tpu as pltpu
from jax.sharding import PartitionSpec as P

HEAD = 128
GROUP = 8
STEPS = 3
ROWS = 8
CACHE = 64
NX = 4
NY = 8
NQ = 16
NT = 8
D_ROWS = 16
ADAPTER_SCALE = 2.0
ROPE_BASE = 1000000.0
MASKED = -1e30
MESH = pl.DeviceIdType.MESH
F32 = jnp.float32
BF16 = jnp.bfloat16
N = STEPS * ROWS
M = STEPS * GROUP * ROWS
SLOTS = ROWS * CACHE
W_PARTS = 8
Y_ORDER = (0, 1, 2, 3, 7, 6, 5, 4)


def iota(shape, dim):
    return lax.broadcasted_iota(jnp.int32, shape, dim)


def dot(a, b):
    return jnp.dot(a, b, preferred_element_type=F32)


def dot_t(a, b):
    return lax.dot_general(a, b, (((1,), (1,)), ((), ())), preferred_element_type=F32)


def stack_steps(ref, columns):
    return jnp.concatenate([ref[s, :, columns].astype(F32) for s in range(STEPS)], axis=0)


def kernel(
    x_hbm,
    len_hbm,
    q_hbm,
    k_hbm,
    v_hbm,
    w_hbm,
    bias_hbm,
    d_hbm,
    u_hbm,
    att_v,
    ent_v,
    x_v,
    len_s,
    q_v,
    k_v,
    v_v,
    w_v,
    bias_v,
    u_v,
    u_own,
    d_all,
    xs,
    xr,
    u1,
    u2,
    pp,
    pr,
    pt,
    xb,
    proj,
    cos_v,
    sin_v,
    qb,
    peak_c,
    total_c,
    acc_c,
    ublk,
    in_sem,
    w_sem,
    d_send,
    d_recv,
    df_sem,
    x_send,
    x_recv,
    u1_send,
    u1_recv,
    uf_sem,
    u2_send,
    u2_recv,
    p_send,
    p_recv,
    t_send,
    t_recv,
    near_in,
    go,
):
    f = lax.axis_index("fsdp")
    t = lax.axis_index("tp")
    q, x = f // NX, lax.rem(f, NX)
    y, half = q // 2, lax.rem(q, 2)
    mirror = (NT // 2 - 1 - t // 2) * 2 + lax.rem(t, 2)
    width = x_v.shape[2]

    def at(yy, hh, xx):
        return (yy * 2 + hh) * NX + xx

    def plus(i, d, n):
        return lax.rem(i + d, n)

    def load(i, src, dst):
        copy = pltpu.make_async_copy(src, dst, in_sem.at[i])
        copy.start()
        return copy

    loads = {
        "u": load(0, u_hbm, u_v),
        "x": load(1, x_hbm, x_v),
        "len": load(2, len_hbm, len_s),
        "bias": load(3, bias_hbm, bias_v),
        "q": load(4, q_hbm, q_v),
        "k": load(5, k_hbm, k_v),
        "v": load(6, v_hbm, v_v),
    }
    d_load = pltpu.make_async_copy(d_hbm, d_all.at[q], in_sem.at[7])
    part = width // W_PARTS

    def w_load(i):
        rows = pl.ds(pl.multiple_of(i * part, part), part)
        return pltpu.make_async_copy(w_hbm.at[:, rows], w_v.at[:, rows], w_sem.at[i])

    def remote(src, dst, send, recv, where):
        return pltpu.make_async_remote_copy(
            src_ref=src, dst_ref=dst, send_sem=send, recv_sem=recv, device_id=where, device_id_type=MESH
        )

    def d_out(yy):
        where = (at(yy, 0, x), jnp.where(half == 0, t, mirror))
        return remote(d_hbm, d_all.at[q], d_send.at[yy], d_recv.at[q], where)

    def d_in(qq):
        return remote(d_hbm, d_all.at[qq], d_send.at[0], d_recv.at[qq], (f, t))

    def u1_out(yy):
        return remote(u_own, u1.at[q], u1_send.at[yy], u1_recv.at[q], (at(yy, 0, x), t))

    def u1_in(qq):
        return remote(u_own, u1.at[qq], u1_send.at[0], u1_recv.at[qq], (f, t))

    def d_over():
        return remote(d_all, d_all, df_sem.at[0], df_sem.at[1], (at(y, 1 - half, x), mirror))

    def u1_over():
        return remote(u1, u1, uf_sem.at[0], uf_sem.at[1], (at(y, 1 - half, x), t))

    def along_x(src, dst, send, recv, d):
        return remote(src, dst, send.at[d], recv.at[d], (at(y, half, plus(x, d, NX)), t))

    def x_copy(d, block):
        return along_x(xs.at[plus(x, d, NX)], xr.at[block], x_send, x_recv, d)

    def p_copy(d, block):
        return along_x(pp.at[plus(x, d, NX)], pr.at[block], p_send, p_recv, d)

    def u2_copy(d, block):
        return along_x(u2.at[block], u2.at[block], u2_send, u2_recv, d)

    def t_copy(d, block):
        return remote(pt.at[block], pt.at[block], t_send.at[d], t_recv.at[d], (f, plus(t, d, NT)))

    def from_x(d):
        return plus(x, NX - d, NX)

    def from_t(d):
        return plus(t, NT - d, NT)

    barrier = pltpu.get_barrier_semaphore()

    def signal(semaphore, where):
        pl.semaphore_signal(semaphore, inc=1, device_id=where, device_id_type=MESH)

    @pl.when(half == 0)
    def _():
        d_load.start()
        for yy in Y_ORDER:
            signal(barrier, (at(yy, 1, x), mirror))
            signal(barrier, (at(yy, 1, x), t))
        for d in range(1, NY):
            signal(barrier, (at(plus(y, d, NY), 0, x), t))
        for d in range(1, NX):
            signal(barrier, (at(y, 0, plus(x, d, NX)), t))
        for d in range(1, NT):
            signal(barrier, (f, plus(t, d, NT)))

    pl.semaphore_wait(barrier, jnp.where(half == 0, NY + NX + NT - 3, 2 * NY))

    @pl.when(half == 1)
    def _():
        for yy in Y_ORDER:
            d_out(yy).start()

    @pl.when(half == 0)
    def _():
        for d in range(1, NY):
            d_out(plus(y, d, NY)).start()

    loads["u"].wait()
    u_own[...] = jnp.concatenate([u_v[0:1].astype(F32), u_v[1:2].astype(F32)], axis=1)

    @pl.when(half == 1)
    def _():
        for yy in Y_ORDER:
            u1_out(yy).start()

    @pl.when(half == 0)
    def _():
        u1[q] = u_own[...]
        for d in range(1, NY):
            u1_out(plus(y, d, NY)).start()

    for i in range(W_PARTS):
        w_load(i).start()

    span = NT * D_ROWS
    per = HEAD // D_ROWS
    groups = NQ // per
    shape = (per * span, HEAD)
    block = iota(shape, 1) // D_ROWS
    owner = jnp.where(lax.rem(block, 2) == half, t, mirror)
    pick = (iota(shape, 0) // span == block) & (
        lax.rem(iota(shape, 0), span) == owner * D_ROWS + lax.rem(iota(shape, 1), D_ROWS)
    )
    pick = jnp.where(pick, 1.0, 0.0).astype(BF16)
    loads["x"].wait()
    rows = []
    for j in range(NX):
        for g in range(groups):
            rows.append(
                jnp.concatenate(
                    [
                        stack_steps(x_v, pl.ds(((g * per + i) * NX + j) * span, span))
                        for i in range(per)
                    ],
                    axis=1,
                )
            )
    picked = dot(jnp.concatenate(rows, axis=0).astype(BF16), pick)
    for j in range(NX):
        for g in range(groups):
            base = (j * groups + g) * N
            for s in range(STEPS):
                xs[j, s, :, g * HEAD : (g + 1) * HEAD] = picked[
                    base + s * ROWS : base + (s + 1) * ROWS
                ].astype(BF16)
    xr[x] = xs[x]
    @pl.when(half == 0)
    def _():
        for d in range(1, NX):
            x_copy(d, x).start()

    for name in ("q", "k", "len"):
        loads[name].wait()
    queries = jnp.concatenate(
        [
            q_v[s, :, h * HEAD : (h + 1) * HEAD].astype(F32)
            for s in range(STEPS)
            for h in range(GROUP)
        ],
        axis=0,
    ).astype(BF16)
    qb[...] = queries
    scale = HEAD**-0.5
    row = iota((ROWS, HEAD), 0)
    length = jnp.zeros((ROWS, HEAD), jnp.int32)
    for b in range(ROWS):
        length = jnp.where(row == b, len_s[b], length)
    column = iota((ROWS, SLOTS), 1)
    valid = (column // CACHE == iota((ROWS, SLOTS), 0)) & (
        lax.rem(column, CACHE) < jnp.concatenate([length] * (SLOTS // HEAD), axis=1)
    )
    scores = dot_t(queries, k_v[...].reshape(SLOTS, HEAD)) * scale
    scores = jnp.where(
        valid[None], scores.reshape(STEPS * GROUP, ROWS, SLOTS), MASKED
    ).reshape(M, SLOTS)
    peak = jnp.max(scores, axis=-1, keepdims=True)
    raised = jnp.exp(scores - peak)
    peak_c[...] = jnp.broadcast_to(peak, (M, HEAD))
    total_c[...] = jnp.broadcast_to(jnp.sum(raised, axis=-1, keepdims=True), (M, HEAD))
    loads["v"].wait()
    acc_c[...] = dot(raised.astype(BF16), v_v[...].reshape(SLOTS, HEAD))

    for s in range(STEPS):
        xb[pl.ds(s * ROWS, ROWS)] = x_v[s].astype(F32)
    proj[...] = jnp.zeros_like(proj)

    def project(i, carry):
        w_load(i).wait()
        rows = pl.ds(pl.multiple_of(i * part, part), part)
        proj[...] += dot(
            xb[:, rows].astype(BF16), jnp.concatenate([w_v[0, rows], w_v[1, rows]], axis=1)
        )
        return carry

    lax.fori_loop(0, W_PARTS, project, 0)

    loads["bias"].wait()
    proj[...] += jnp.concatenate([bias_v[0:1], bias_v[1:2]], axis=1).astype(F32)
    turn = HEAD // 2
    lane = iota((ROWS, HEAD), 1)
    frequency = jnp.exp(lax.rem(lane, turn).astype(F32) * (-2.0 / HEAD * math.log(ROPE_BASE)))
    for s in range(STEPS):
        angle = (length + s).astype(F32) * frequency
        cos_v[pl.ds(s * ROWS, ROWS)] = jnp.cos(angle)
        sine = jnp.sin(angle)
        sin_v[pl.ds(s * ROWS, ROWS)] = jnp.where(lane < turn, -sine, sine)

    @pl.when(half == 0)
    def _():
        d_load.wait()
        d_in(q + 1).wait_recv()
        for d in range(1, NX):
            signal(near_in, (at(y, 0, plus(x, d, NX)), t))
        for d in range(1, NT):
            signal(near_in, (f, plus(t, d, NT)))
        pl.semaphore_wait(near_in, NX + NT - 2)
        signal(go, (at(y, 1, x), mirror))
        for d in range(1, NY):
            d_in(plus(y, d, NY) * 2).wait_recv()
            d_in(plus(y, d, NY) * 2 + 1).wait_recv()

    @pl.when(half == 1)
    def _():
        pl.semaphore_wait(go, 1)
        for d in range(1, NX):
            x_copy(d, x).start()
        d_over().wait_recv()

    for d in range(1, NX):
        x_copy(d, from_x(d)).wait_recv()
    mine = jnp.concatenate([stack_steps(xr.at[j], slice(None)) for j in range(NX)], axis=0)
    partial = dot(mine.astype(BF16), d_all[...].reshape(NQ * D_ROWS, HEAD))
    for j in range(NX):
        for s in range(STEPS):
            base = j * N + s * ROWS
            pp[j, s] = partial[base : base + ROWS]
    for d in range(1, NX):
        p_copy(d, x).start()
    pr[x] = pp[x]

    @pl.when(half == 0)
    def _():
        d_over().start()
        for d in range(1, NY):
            u1_in(plus(y, d, NY) * 2).wait_recv()
        for yy in range(NY):
            u1_in(yy * 2 + 1).wait_recv()
        u1_over().start()

    @pl.when(half == 1)
    def _():
        u1_over().wait_recv()

    u2[x] = u1[...].reshape(NQ, 2 * HEAD).astype(BF16)
    for d in range(1, NX):
        u2_copy(d, x).start()

    for d in range(1, NX):
        p_copy(d, from_x(d)).wait_recv()
    for s in range(STEPS):
        pt[t, s] = pr[0, s] + pr[1, s] + pr[2, s] + pr[3, s]
    for d in range(1, NT):
        t_copy(d, t).start()

    for d in range(1, NX):
        u2_copy(d, from_x(d)).wait_recv()
    ranks = NQ * NX
    order = iota((ranks, ranks), 0)
    order = iota((ranks, ranks), 1) == lax.rem(order, NX) * NQ + order // NX
    up = dot(jnp.where(order, 1.0, 0.0).astype(BF16), u2[...].reshape(ranks, 2 * HEAD))
    up = up * ADAPTER_SCALE
    which = iota((ranks, 2 * HEAD), 1) < HEAD
    ublk[...] = jnp.concatenate(
        [jnp.where(which, up, 0.0), jnp.where(which, 0.0, up)], axis=0
    ).astype(BF16)

    @pl.when(half == 0)
    def _():
        for d in range(1, NY):
            d_out(plus(y, d, NY)).wait_send()
            u1_out(plus(y, d, NY)).wait_send()
        d_over().wait_send()
        u1_over().wait_send()

    @pl.when(half == 1)
    def _():
        for yy in range(NY):
            d_out(yy).wait_send()
            u1_out(yy).wait_send()

    for d in range(1, NX):
        x_copy(d, x).wait_send()
        p_copy(d, x).wait_send()
        u2_copy(d, x).wait_send()

    for d in range(1, NT):
        t_copy(d, from_t(d)).wait_recv()
    sums = []
    for s in range(STEPS):
        total = pt[0, s]
        for i in range(1, NT):
            total = total + pt[i, s]
        sums.append(total)
    low_rank = jnp.concatenate(sums, axis=0)
    high = low_rank.astype(BF16).astype(F32)
    both = jnp.concatenate([high, low_rank - high], axis=0).astype(BF16)
    change = dot(both, ublk[...])
    fresh = proj[...] + change[:N] + change[N:]
    key = fresh[:, :HEAD]
    key = key * cos_v[...] + pltpu.roll(key, turn, axis=1) * sin_v[...]
    value = fresh[:, HEAD:]
    for s in range(STEPS):
        ent_v[0, s] = key[s * ROWS : (s + 1) * ROWS].astype(BF16)
        ent_v[1, s] = value[s * ROWS : (s + 1) * ROWS].astype(BF16)
    scores = dot_t(qb[...], key.astype(BF16)) * scale
    r, c = iota((M, N), 0), iota((M, N), 1)
    scores = jnp.where(
        (lax.rem(r, ROWS) == lax.rem(c, ROWS)) & (c // ROWS <= r // (GROUP * ROWS)), scores, MASKED
    )
    peak_old = peak_c[:, 0:1]
    peak = jnp.maximum(peak_old, jnp.max(scores, axis=-1, keepdims=True))
    raised = jnp.exp(scores - peak)
    shrink = jnp.exp(peak_old - peak)
    total = shrink * total_c[:, 0:1] + jnp.sum(raised, axis=-1, keepdims=True)
    out = (shrink * acc_c[...] + dot(raised.astype(BF16), value.astype(BF16))) / total
    for s in range(STEPS):
        for h in range(GROUP):
            base = (s * GROUP + h) * ROWS
            att_v[s, :, h * HEAD : (h + 1) * HEAD] = out[base : base + ROWS].astype(BF16)

    for d in range(1, NT):
        t_copy(d, t).wait_send()


def deliver(att_v, ent_v, att_hbm, ent_hbm, sem):
    copies = [
        pltpu.make_async_copy(att_v, att_hbm, sem.at[0]),
        pltpu.make_async_copy(ent_v, ent_hbm, sem.at[1]),
    ]
    for copy in copies:
        copy.start()
    for copy in copies:
        copy.wait()


def body(x, lengths, queries, keys, values, weight, bias, down, up):
    width = x.shape[2]
    vmem = pltpu.VMEM
    dma = pltpu.SemaphoreType.DMA
    anywhere = pl.BlockSpec(memory_space=pl.ANY)
    inside = pl.BlockSpec(memory_space=pltpu.VMEM)
    entries = (2, STEPS, ROWS, HEAD)
    attended, entry = pl.pallas_call(
        kernel,
        out_shape=(pltpu.VMEM(queries.shape, BF16), pltpu.VMEM(entries, BF16)),
        in_specs=[anywhere] * 9,
        out_specs=(inside, inside),
        scratch_shapes=[
            vmem(x.shape, BF16),
            pltpu.SMEM(lengths.shape, jnp.int32),
            vmem(queries.shape, BF16),
            vmem(keys.shape, BF16),
            vmem(values.shape, BF16),
            vmem(weight.shape, BF16),
            vmem(bias.shape, BF16),
            vmem((2, HEAD), BF16),
            vmem((1, 2 * HEAD), F32),
            vmem((NQ, D_ROWS, HEAD), BF16),
            vmem((NX, STEPS, ROWS, NQ * D_ROWS), BF16),
            vmem((NX, STEPS, ROWS, NQ * D_ROWS), BF16),
            vmem((NQ, 1, 2 * HEAD), F32),
            vmem((NX, NQ, 2 * HEAD), BF16),
            vmem((NX, STEPS, ROWS, HEAD), F32),
            vmem((NX, STEPS, ROWS, HEAD), F32),
            vmem((NT, STEPS, ROWS, HEAD), F32),
            vmem((N, width), F32),
            vmem((N, 2 * HEAD), F32),
            vmem((N, HEAD), F32),
            vmem((N, HEAD), F32),
            vmem((M, HEAD), BF16),
            vmem((M, HEAD), F32),
            vmem((M, HEAD), F32),
            vmem((M, HEAD), F32),
            vmem((2 * NQ * NX, 2 * HEAD), BF16),
            dma((8,)),
            dma((W_PARTS,)),
            dma((NY,)),
            dma((NQ,)),
            dma((2,)),
            dma((NX,)),
            dma((NX,)),
            dma((NY,)),
            dma((NQ,)),
            dma((2,)),
            dma((NX,)),
            dma((NX,)),
            dma((NX,)),
            dma((NX,)),
            dma((NT,)),
            dma((NT,)),
            pltpu.SemaphoreType.REGULAR,
            pltpu.SemaphoreType.REGULAR,
        ],
        compiler_params=pltpu.CompilerParams(
            collective_id=0, has_side_effects=True, vmem_limit_bytes=60 * 1024 * 1024
        ),
        name="adapter_attention",
    )(x, lengths, queries, keys, values, weight, bias, down, up.reshape(2, HEAD))
    return pl.pallas_call(
        deliver,
        out_shape=(
            jax.ShapeDtypeStruct(queries.shape, BF16),
            jax.ShapeDtypeStruct(entries, BF16),
        ),
        in_specs=[inside] * 2,
        out_specs=(anywhere, anywhere),
        scratch_shapes=[dma((2,))],
        compiler_params=pltpu.CompilerParams(vmem_limit_bytes=1024 * 1024),
        name="deliver",
    )(attended, entry)


def solution(mesh):
    placed = (
        P(None, "fsdp", None),
        P("fsdp"),
        P(None, "fsdp", "tp"),
        P("fsdp", None, "tp"),
        P("fsdp", None, "tp"),
        P(None, None, "tp"),
        P(None, "tp"),
        P(("fsdp", "tp"), None),
        P(None, "fsdp", "tp"),
    )
    return jax.shard_map(
        body,
        mesh=mesh,
        in_specs=placed,
        out_specs=(P(None, "fsdp", "tp"), P(None, None, "fsdp", "tp")),
        check_vma=False,
    )
```

```python
import math

import jax
import jax.numpy as jnp
from jax import lax
from jax.experimental import pallas as pl
from jax.experimental.pallas import tpu as pltpu
from jax.sharding import PartitionSpec as P

HEAD = 128
GROUP = 8
STEPS = 3
ROWS = 8
CACHE = 64
NX = 4
NY = 8
NQ = 16
NT = 8
D_ROWS = 16
ADAPTER_SCALE = 2.0
ROPE_BASE = 1000000.0
MASKED = -1e30
MESH = pl.DeviceIdType.MESH
F32 = jnp.float32
BF16 = jnp.bfloat16
N = STEPS * ROWS
M = STEPS * GROUP * ROWS
SLOTS = ROWS * CACHE
W_PARTS = 8
Y_ORDER = (0, 1, 2, 3, 7, 6, 5, 4)


def iota(shape, dim):
    return lax.broadcasted_iota(jnp.int32, shape, dim)


def dot(a, b):
    return jnp.dot(a, b, preferred_element_type=F32)


def dot_t(a, b):
    return lax.dot_general(a, b, (((1,), (1,)), ((), ())), preferred_element_type=F32)


def stack_steps(ref, columns):
    return jnp.concatenate([ref[s, :, columns].astype(F32) for s in range(STEPS)], axis=0)


def kernel(
    x_hbm,
    len_hbm,
    q_hbm,
    k_hbm,
    v_hbm,
    w_hbm,
    bias_hbm,
    d_hbm,
    u_hbm,
    att_v,
    ent_v,
    x_v,
    len_s,
    q_v,
    k_v,
    v_v,
    w_v,
    bias_v,
    u_v,
    u_own,
    d_all,
    xs,
    xr,
    x_all,
    u1,
    u2,
    pp,
    pr,
    pt,
    xb,
    proj,
    cos_v,
    sin_v,
    qb,
    peak_c,
    total_c,
    acc_c,
    ublk,
    in_sem,
    w_sem,
    d_send,
    d_recv,
    df_sem,
    x_send,
    x_recv,
    u1_send,
    u1_recv,
    uf_sem,
    u2_send,
    u2_recv,
    p_send,
    p_recv,
    t_send,
    t_recv,
    near_x,
    near_t,
    go_x,
    go_t,
):
    f = lax.axis_index("fsdp")
    t = lax.axis_index("tp")
    q, x = f // NX, lax.rem(f, NX)
    y, half = q // 2, lax.rem(q, 2)
    mirror = (NT // 2 - 1 - t // 2) * 2 + lax.rem(t, 2)
    width = x_v.shape[2]

    def at(yy, hh, xx):
        return (yy * 2 + hh) * NX + xx

    def plus(i, d, n):
        return lax.rem(i + d, n)

    def load(i, src, dst):
        return pltpu.make_async_copy(src, dst, in_sem.at[i])

    loads = {
        "u": load(0, u_hbm, u_v),
        "x": load(1, x_hbm, x_v),
        "len": load(2, len_hbm, len_s),
        "bias": load(3, bias_hbm, bias_v),
        "q": load(4, q_hbm, q_v),
        "k": load(5, k_hbm, k_v),
        "v": load(6, v_hbm, v_v),
    }
    d_load = pltpu.make_async_copy(d_hbm, d_all.at[q], in_sem.at[7])
    part = width // W_PARTS

    def w_load(i):
        rows = pl.ds(pl.multiple_of(i * part, part), part)
        return pltpu.make_async_copy(w_hbm.at[:, rows], w_v.at[:, rows], w_sem.at[i])

    def remote(src, dst, send, recv, where):
        return pltpu.make_async_remote_copy(
            src_ref=src, dst_ref=dst, send_sem=send, recv_sem=recv, device_id=where, device_id_type=MESH
        )

    def d_out(yy):
        where = (at(yy, 0, x), jnp.where(half == 0, t, mirror))
        return remote(d_hbm, d_all.at[q], d_send.at[yy], d_recv.at[q], where)

    def d_in(qq):
        return remote(d_hbm, d_all.at[qq], d_send.at[0], d_recv.at[qq], (f, t))

    def u1_out(yy):
        return remote(u_own, u1.at[q], u1_send.at[yy], u1_recv.at[q], (at(yy, 0, x), t))

    def u1_in(qq):
        return remote(u_own, u1.at[qq], u1_send.at[0], u1_recv.at[qq], (f, t))

    def d_over():
        return remote(d_all, d_all, df_sem.at[0], df_sem.at[1], (at(y, 1 - half, x), mirror))

    def u1_over():
        return remote(u1, u1, uf_sem.at[0], uf_sem.at[1], (at(y, 1 - half, x), t))

    def along_x(src, dst, send, recv, d):
        return remote(src, dst, send.at[d], recv.at[d], (at(y, half, plus(x, d, NX)), t))

    def x_copy(d, block):
        return along_x(xs.at[plus(x, d, NX)], xr.at[block], x_send, x_recv, d)

    def p_copy(d, block):
        return along_x(pp.at[plus(x, d, NX)], pr.at[block], p_send, p_recv, d)

    def u2_copy(d, block):
        return along_x(u2.at[block], u2.at[block], u2_send, u2_recv, d)

    def t_out(to):
        return remote(pt.at[t], pt.at[t], t_send.at[to], t_recv.at[t], (f, to))

    def t_in(by):
        return remote(pt.at[by], pt.at[by], t_send.at[by], t_recv.at[by], (f, by))

    def from_x(d):
        return plus(x, NX - d, NX)

    def from_t(d):
        return plus(t, NT - d, NT)

    barrier = pltpu.get_barrier_semaphore()

    def signal(semaphore, where):
        pl.semaphore_signal(semaphore, inc=1, device_id=where, device_id_type=MESH)

    @pl.when(half == 0)
    def _():
        d_load.start()
        for yy in Y_ORDER:
            signal(barrier, (at(yy, 1, x), mirror))
            signal(barrier, (at(yy, 1, x), t))
        for d in range(1, NY):
            signal(barrier, (at(plus(y, d, NY), 0, x), t))
        for d in range(1, NX):
            signal(barrier, (at(y, 0, plus(x, d, NX)), t))
        for d in range(1, NT):
            signal(barrier, (f, plus(t, d, NT)))

    @pl.when(half == 1)
    def _():
        pl.semaphore_wait(barrier, 2 * NY)
        for yy in Y_ORDER:
            d_out(yy).start()

    for copy in loads.values():
        copy.start()

    @pl.when(half == 0)
    def _():
        pl.semaphore_wait(barrier, NY + NX + NT - 3)
        for d in range(1, NY):
            d_out(plus(y, d, NY)).start()

    loads["u"].wait()
    u_own[...] = jnp.concatenate([u_v[0:1].astype(F32), u_v[1:2].astype(F32)], axis=1)

    @pl.when(half == 1)
    def _():
        for yy in Y_ORDER:
            u1_out(yy).start()

    @pl.when(half == 0)
    def _():
        u1[q] = u_own[...]
        for d in range(1, NY):
            u1_out(plus(y, d, NY)).start()

    for i in range(W_PARTS):
        w_load(i).start()

    span = NT * D_ROWS
    per = HEAD // D_ROWS
    groups = NQ // per
    shape = (per * span, HEAD)
    block = iota(shape, 1) // D_ROWS
    owner = jnp.where(lax.rem(block, 2) == half, t, mirror)
    pick = (iota(shape, 0) // span == block) & (
        lax.rem(iota(shape, 0), span) == owner * D_ROWS + lax.rem(iota(shape, 1), D_ROWS)
    )
    pick = jnp.where(pick, 1.0, 0.0).astype(BF16)
    loads["x"].wait()
    rows = []
    for j in range(NX):
        for g in range(groups):
            rows.append(
                jnp.concatenate(
                    [
                        stack_steps(x_v, pl.ds(((g * per + i) * NX + j) * span, span))
                        for i in range(per)
                    ],
                    axis=1,
                )
            )
    picked = dot(jnp.concatenate(rows, axis=0).astype(BF16), pick)
    for j in range(NX):
        for g in range(groups):
            base = (j * groups + g) * N
            for s in range(STEPS):
                xs[j, s, :, g * HEAD : (g + 1) * HEAD] = picked[
                    base + s * ROWS : base + (s + 1) * ROWS
                ].astype(BF16)
    xr[x] = xs[x]
    @pl.when(half == 0)
    def _():
        for d in range(1, NX):
            x_copy(d, x).start()

    for name in ("q", "k", "len"):
        loads[name].wait()
    queries = jnp.concatenate(
        [
            q_v[s, :, h * HEAD : (h + 1) * HEAD].astype(F32)
            for s in range(STEPS)
            for h in range(GROUP)
        ],
        axis=0,
    ).astype(BF16)
    qb[...] = queries
    scale = HEAD**-0.5
    row = iota((ROWS, HEAD), 0)
    length = jnp.zeros((ROWS, HEAD), jnp.int32)
    for b in range(ROWS):
        length = jnp.where(row == b, len_s[b], length)
    column = iota((ROWS, SLOTS), 1)
    valid = (column // CACHE == iota((ROWS, SLOTS), 0)) & (
        lax.rem(column, CACHE) < jnp.concatenate([length] * (SLOTS // HEAD), axis=1)
    )
    scores = dot_t(queries, k_v[...].reshape(SLOTS, HEAD)) * scale
    scores = jnp.where(
        valid[None], scores.reshape(STEPS * GROUP, ROWS, SLOTS), MASKED
    ).reshape(M, SLOTS)
    peak = jnp.max(scores, axis=-1, keepdims=True)
    raised = jnp.exp(scores - peak)
    peak_c[...] = jnp.broadcast_to(peak, (M, HEAD))
    total_c[...] = jnp.broadcast_to(jnp.sum(raised, axis=-1, keepdims=True), (M, HEAD))
    loads["v"].wait()
    acc_c[...] = dot(raised.astype(BF16), v_v[...].reshape(SLOTS, HEAD))

    for s in range(STEPS):
        xb[pl.ds(s * ROWS, ROWS)] = x_v[s].astype(F32)
    proj[...] = jnp.zeros_like(proj)

    def project(i, carry):
        w_load(i).wait()
        rows = pl.ds(pl.multiple_of(i * part, part), part)
        proj[...] += dot(
            xb[:, rows].astype(BF16), jnp.concatenate([w_v[0, rows], w_v[1, rows]], axis=1)
        )
        return carry

    lax.fori_loop(0, W_PARTS, project, 0)

    loads["bias"].wait()
    proj[...] += jnp.concatenate([bias_v[0:1], bias_v[1:2]], axis=1).astype(F32)
    turn = HEAD // 2
    lane = iota((ROWS, HEAD), 1)
    frequency = jnp.exp(lax.rem(lane, turn).astype(F32) * (-2.0 / HEAD * math.log(ROPE_BASE)))
    for s in range(STEPS):
        angle = (length + s).astype(F32) * frequency
        cos_v[pl.ds(s * ROWS, ROWS)] = jnp.cos(angle)
        sine = jnp.sin(angle)
        sin_v[pl.ds(s * ROWS, ROWS)] = jnp.where(lane < turn, -sine, sine)

    def gather_x():
        x_all[...] = jnp.concatenate(
            [stack_steps(xr.at[j], slice(None)) for j in range(NX)], axis=0
        ).astype(BF16)

    @pl.when(half == 0)
    def _():
        d_load.wait()
        d_in(q + 1).wait_recv()
        for d in range(1, NX):
            signal(near_x, (at(y, 0, plus(x, d, NX)), t))
        for d in range(1, NT):
            signal(near_t, (f, plus(t, d, NT)))
        pl.semaphore_wait(near_x, NX - 1)
        signal(go_x, (at(y, 1, x), mirror))
        for d in range(1, NX):
            x_copy(d, from_x(d)).wait_recv()
        gather_x()
        for d in range(1, NY):
            d_in(plus(y, d, NY) * 2).wait_recv()
            d_in(plus(y, d, NY) * 2 + 1).wait_recv()

    @pl.when(half == 1)
    def _():
        pl.semaphore_wait(go_x, 1)
        for d in range(1, NX):
            x_copy(d, x).start()
        for d in range(1, NX):
            x_copy(d, from_x(d)).wait_recv()
        gather_x()
        d_over().wait_recv()

    partial = dot(x_all[...], d_all[...].reshape(NQ * D_ROWS, HEAD))
    for j in range(NX):
        for s in range(STEPS):
            base = j * N + s * ROWS
            pp[j, s] = partial[base : base + ROWS]
    for d in (2, 1, 3):
        p_copy(d, x).start()
    pr[x] = pp[x]

    @pl.when(half == 0)
    def _():
        d_over().start()
        pl.semaphore_wait(near_t, NT - 1)
        signal(go_t, (at(y, 1, x), mirror))
        for d in range(1, NY):
            u1_in(plus(y, d, NY) * 2).wait_recv()
        for yy in range(NY):
            u1_in(yy * 2 + 1).wait_recv()
        u1_over().start()

    @pl.when(half == 1)
    def _():
        u1_over().wait_recv()

    u2[x] = u1[...].reshape(NQ, 2 * HEAD).astype(BF16)
    for d in range(1, NX):
        u2_copy(d, x).start()

    for d in range(1, NX):
        p_copy(d, from_x(d)).wait_recv()
    for s in range(STEPS):
        pt[t, s] = pr[0, s] + pr[1, s] + pr[2, s] + pr[3, s]

    @pl.when(half == 1)
    def _():
        pl.semaphore_wait(go_t, 1)

    for to in range(NT):

        @pl.when(t != to)
        def _(to=to):
            t_out(to).start()

    for d in range(1, NX):
        u2_copy(d, from_x(d)).wait_recv()
    ranks = NQ * NX
    order = iota((ranks, ranks), 0)
    order = iota((ranks, ranks), 1) == lax.rem(order, NX) * NQ + order // NX
    up = dot(jnp.where(order, 1.0, 0.0).astype(BF16), u2[...].reshape(ranks, 2 * HEAD))
    up = up * ADAPTER_SCALE
    which = iota((ranks, 2 * HEAD), 1) < HEAD
    ublk[...] = jnp.concatenate(
        [jnp.where(which, up, 0.0), jnp.where(which, 0.0, up)], axis=0
    ).astype(BF16)

    @pl.when(half == 0)
    def _():
        for d in range(1, NY):
            d_out(plus(y, d, NY)).wait_send()
            u1_out(plus(y, d, NY)).wait_send()
        d_over().wait_send()
        u1_over().wait_send()

    @pl.when(half == 1)
    def _():
        for yy in range(NY):
            d_out(yy).wait_send()
            u1_out(yy).wait_send()

    for d in range(1, NX):
        x_copy(d, x).wait_send()
        p_copy(d, x).wait_send()
        u2_copy(d, x).wait_send()

    for d in range(1, NT):
        t_in(from_t(d)).wait_recv()
    sums = []
    for s in range(STEPS):
        total = pt[0, s]
        for i in range(1, NT):
            total = total + pt[i, s]
        sums.append(total)
    low_rank = jnp.concatenate(sums, axis=0)
    high = low_rank.astype(BF16).astype(F32)
    both = jnp.concatenate([high, low_rank - high], axis=0).astype(BF16)
    change = dot(both, ublk[...])
    fresh = proj[...] + change[:N] + change[N:]
    key = fresh[:, :HEAD]
    key = key * cos_v[...] + pltpu.roll(key, turn, axis=1) * sin_v[...]
    value = fresh[:, HEAD:]
    for s in range(STEPS):
        ent_v[0, s] = key[s * ROWS : (s + 1) * ROWS].astype(BF16)
        ent_v[1, s] = value[s * ROWS : (s + 1) * ROWS].astype(BF16)
    scores = dot_t(qb[...], key.astype(BF16)) * scale
    r, c = iota((M, N), 0), iota((M, N), 1)
    scores = jnp.where(
        (lax.rem(r, ROWS) == lax.rem(c, ROWS)) & (c // ROWS <= r // (GROUP * ROWS)), scores, MASKED
    )
    peak_old = peak_c[:, 0:1]
    peak = jnp.maximum(peak_old, jnp.max(scores, axis=-1, keepdims=True))
    raised = jnp.exp(scores - peak)
    shrink = jnp.exp(peak_old - peak)
    total = shrink * total_c[:, 0:1] + jnp.sum(raised, axis=-1, keepdims=True)
    out = (shrink * acc_c[...] + dot(raised.astype(BF16), value.astype(BF16))) / total
    for s in range(STEPS):
        for h in range(GROUP):
            base = (s * GROUP + h) * ROWS
            att_v[s, :, h * HEAD : (h + 1) * HEAD] = out[base : base + ROWS].astype(BF16)

    for d in range(1, NT):
        t_out(from_t(d)).wait_send()


def deliver(att_v, ent_v, att_hbm, ent_hbm, sem):
    copies = [
        pltpu.make_async_copy(att_v, att_hbm, sem.at[0]),
        pltpu.make_async_copy(ent_v, ent_hbm, sem.at[1]),
    ]
    for copy in copies:
        copy.start()
    for copy in copies:
        copy.wait()


def body(x, lengths, queries, keys, values, weight, bias, down, up):
    width = x.shape[2]
    vmem = pltpu.VMEM
    dma = pltpu.SemaphoreType.DMA
    anywhere = pl.BlockSpec(memory_space=pl.ANY)
    inside = pl.BlockSpec(memory_space=pltpu.VMEM)
    entries = (2, STEPS, ROWS, HEAD)
    attended, entry = pl.pallas_call(
        kernel,
        out_shape=(pltpu.VMEM(queries.shape, BF16), pltpu.VMEM(entries, BF16)),
        in_specs=[anywhere] * 9,
        out_specs=(inside, inside),
        scratch_shapes=[
            vmem(x.shape, BF16),
            pltpu.SMEM(lengths.shape, jnp.int32),
            vmem(queries.shape, BF16),
            vmem(keys.shape, BF16),
            vmem(values.shape, BF16),
            vmem(weight.shape, BF16),
            vmem(bias.shape, BF16),
            vmem((2, HEAD), BF16),
            vmem((1, 2 * HEAD), F32),
            vmem((NQ, D_ROWS, HEAD), BF16),
            vmem((NX, STEPS, ROWS, NQ * D_ROWS), BF16),
            vmem((NX, STEPS, ROWS, NQ * D_ROWS), BF16),
            vmem((NX * N, NQ * D_ROWS), BF16),
            vmem((NQ, 1, 2 * HEAD), F32),
            vmem((NX, NQ, 2 * HEAD), BF16),
            vmem((NX, STEPS, ROWS, HEAD), F32),
            vmem((NX, STEPS, ROWS, HEAD), F32),
            vmem((NT, STEPS, ROWS, HEAD), F32),
            vmem((N, width), F32),
            vmem((N, 2 * HEAD), F32),
            vmem((N, HEAD), F32),
            vmem((N, HEAD), F32),
            vmem((M, HEAD), BF16),
            vmem((M, HEAD), F32),
            vmem((M, HEAD), F32),
            vmem((M, HEAD), F32),
            vmem((2 * NQ * NX, 2 * HEAD), BF16),
            dma((8,)),
            dma((W_PARTS,)),
            dma((NY,)),
            dma((NQ,)),
            dma((2,)),
            dma((NX,)),
            dma((NX,)),
            dma((NY,)),
            dma((NQ,)),
            dma((2,)),
            dma((NX,)),
            dma((NX,)),
            dma((NX,)),
            dma((NX,)),
            dma((NT,)),
            dma((NT,)),
            pltpu.SemaphoreType.REGULAR,
            pltpu.SemaphoreType.REGULAR,
            pltpu.SemaphoreType.REGULAR,
            pltpu.SemaphoreType.REGULAR,
        ],
        compiler_params=pltpu.CompilerParams(
            collective_id=0, has_side_effects=True, vmem_limit_bytes=60 * 1024 * 1024
        ),
        name="adapter_attention",
    )(x, lengths, queries, keys, values, weight, bias, down, up.reshape(2, HEAD))
    return pl.pallas_call(
        deliver,
        out_shape=(
            jax.ShapeDtypeStruct(queries.shape, BF16),
            jax.ShapeDtypeStruct(entries, BF16),
        ),
        in_specs=[inside] * 2,
        out_specs=(anywhere, anywhere),
        scratch_shapes=[dma((2,))],
        compiler_params=pltpu.CompilerParams(vmem_limit_bytes=1024 * 1024),
        name="deliver",
    )(attended, entry)


def solution(mesh):
    placed = (
        P(None, "fsdp", None),
        P("fsdp"),
        P(None, "fsdp", "tp"),
        P("fsdp", None, "tp"),
        P("fsdp", None, "tp"),
        P(None, None, "tp"),
        P(None, "tp"),
        P(("fsdp", "tp"), None),
        P(None, "fsdp", "tp"),
    )
    return jax.shard_map(
        body,
        mesh=mesh,
        in_specs=placed,
        out_specs=(P(None, "fsdp", "tp"), P(None, None, "fsdp", "tp")),
        check_vma=False,
    )
```

```python
import math

import jax
import jax.numpy as jnp
from jax import lax
from jax.experimental import pallas as pl
from jax.experimental.pallas import tpu as pltpu
from jax.sharding import PartitionSpec as P

HEAD = 128
GROUP = 8
STEPS = 3
ROWS = 8
CACHE = 64
NX = 4
NY = 8
NQ = 16
NT = 8
D_ROWS = 16
ADAPTER_SCALE = 2.0
ROPE_BASE = 1000000.0
MASKED = -1e30
MESH = pl.DeviceIdType.MESH
F32 = jnp.float32
BF16 = jnp.bfloat16
N = STEPS * ROWS
M = STEPS * GROUP * ROWS
SLOTS = ROWS * CACHE
W_PARTS = 8
T_ORDER = (1, 0, 3, 2, 5, 4, 7, 6)
Y_ORDER = (0, 1, 2, 3, 7, 6, 5, 4)


def iota(shape, dim):
    return lax.broadcasted_iota(jnp.int32, shape, dim)


def dot(a, b):
    return jnp.dot(a, b, preferred_element_type=F32)


def dot_t(a, b):
    return lax.dot_general(a, b, (((1,), (1,)), ((), ())), preferred_element_type=F32)


def stack_steps(ref, columns):
    return jnp.concatenate([ref[s, :, columns].astype(F32) for s in range(STEPS)], axis=0)


def kernel(
    x_hbm,
    len_hbm,
    q_hbm,
    k_hbm,
    v_hbm,
    w_hbm,
    bias_hbm,
    d_hbm,
    u_hbm,
    att_v,
    ent_v,
    x_v,
    len_s,
    q_v,
    k_v,
    v_v,
    w_v,
    bias_v,
    u_v,
    u_own,
    d_all,
    xs,
    xr,
    x_all,
    u_all,
    u_far,
    pp,
    pr,
    pt,
    xb,
    proj,
    cos_v,
    sin_v,
    qb,
    peak_c,
    total_c,
    acc_c,
    ublk,
    in_sem,
    w_sem,
    d_send,
    d_recv,
    df_sem,
    x_send,
    x_recv,
    u1_send,
    u1_recv,
    uh_send,
    uh_recv,
    ub_send,
    ub_recv,
    u2_send,
    u2_recv,
    p_send,
    p_recv,
    t_send,
    t_recv,
    near_x,
    near_t,
    go_x,
    go_t,
):
    f = lax.axis_index("fsdp")
    t = lax.axis_index("tp")
    q, x = f // NX, lax.rem(f, NX)
    y, half = q // 2, lax.rem(q, 2)
    mirror = (NT // 2 - 1 - t // 2) * 2 + lax.rem(t, 2)
    width = x_v.shape[2]

    def at(yy, hh, xx):
        return (yy * 2 + hh) * NX + xx

    def plus(i, d, n):
        return lax.rem(i + d, n)

    def load(i, src, dst):
        return pltpu.make_async_copy(src, dst, in_sem.at[i])

    loads = {
        "u": load(0, u_hbm, u_v),
        "x": load(1, x_hbm, x_v),
        "len": load(2, len_hbm, len_s),
        "bias": load(3, bias_hbm, bias_v),
        "q": load(4, q_hbm, q_v),
        "k": load(5, k_hbm, k_v),
        "v": load(6, v_hbm, v_v),
    }
    d_load = pltpu.make_async_copy(d_hbm, d_all.at[q], in_sem.at[7])
    part = width // W_PARTS

    def w_load(i):
        rows = pl.ds(pl.multiple_of(i * part, part), part)
        return pltpu.make_async_copy(w_hbm.at[:, rows], w_v.at[:, rows], w_sem.at[i])

    def remote(src, dst, send, recv, where):
        return pltpu.make_async_remote_copy(
            src_ref=src, dst_ref=dst, send_sem=send, recv_sem=recv, device_id=where, device_id_type=MESH
        )

    def d_out(yy):
        where = (at(yy, 0, x), jnp.where(half == 0, t, mirror))
        return remote(d_hbm, d_all.at[q], d_send.at[yy], d_recv.at[q], where)

    def d_in(qq):
        return remote(d_hbm, d_all.at[qq], d_send.at[0], d_recv.at[qq], (f, t))

    def u_out(yy):
        where = (at(yy, 0, x), t)
        return remote(u_own, u_all.at[x, 0, y], u1_send.at[yy], u1_recv.at[y, 0], where)

    def u_out_over(yy):
        where = (at(yy, 0, x), mirror)
        return remote(u_own, u_far.at[y], u1_send.at[yy], u1_recv.at[y, 1], where)

    def u_in(yy):
        return remote(u_own, u_all.at[x, 0, yy], u1_send.at[0], u1_recv.at[yy, 0], (f, t))

    def u_in_over(yy):
        return remote(u_own, u_far.at[yy], u1_send.at[0], u1_recv.at[yy, 1], (f, t))

    def u_home(xx):
        where = (at(y, 0, xx), mirror)
        return remote(u_far, u_all.at[x, 1], uh_send.at[xx], uh_recv.at[x], where)

    def u_home_in(xx):
        return remote(u_far, u_all.at[xx, 1], uh_send.at[xx], uh_recv.at[xx], (f, t))

    def u_back(h):
        source, to = ((u_all.at[x, 0], t), (u_far, mirror))[h]
        return remote(source, u_all.at[x, h], ub_send.at[h], ub_recv.at[h], (at(y, 1, x), to))

    def d_over():
        return remote(d_all, d_all, df_sem.at[0], df_sem.at[1], (at(y, 1 - half, x), mirror))

    def along_x(src, dst, send, recv, d):
        return remote(src, dst, send.at[d], recv.at[d], (at(y, half, plus(x, d, NX)), t))

    def x_copy(d, block):
        return along_x(xs.at[plus(x, d, NX)], xr.at[block], x_send, x_recv, d)

    def p_copy(d, block):
        return along_x(pp.at[plus(x, d, NX)], pr.at[block], p_send, p_recv, d)

    def u2_half(d, block):
        return along_x(u_all.at[block, 0], u_all.at[block, 0], u2_send, u2_recv, d)

    def u2_both(d, block):
        return along_x(u_all.at[block], u_all.at[block], u2_send, u2_recv, d)

    def t_out(to):
        return remote(pt.at[t], pt.at[t], t_send.at[to], t_recv.at[t], (f, to))

    def t_in(by):
        return remote(pt.at[by], pt.at[by], t_send.at[by], t_recv.at[by], (f, by))

    def from_x(d):
        return plus(x, NX - d, NX)

    def from_t(d):
        return plus(t, NT - d, NT)

    loads["u"].start()

    barrier = pltpu.get_barrier_semaphore()

    def signal(semaphore, where):
        pl.semaphore_signal(semaphore, inc=1, device_id=where, device_id_type=MESH)

    @pl.when(half == 0)
    def _():
        d_load.start()
        for yy in Y_ORDER:
            signal(barrier, (at(yy, 1, x), mirror))
        for d in range(1, NY):
            signal(barrier, (at(plus(y, d, NY), 0, x), t))
        for d in range(1, NX):
            signal(barrier, (at(y, 0, plus(x, d, NX)), t))
        for d in range(1, NT):
            signal(barrier, (f, plus(t, d, NT)))

    @pl.when(half == 1)
    def _():
        pl.semaphore_wait(barrier, NY)
        for yy in Y_ORDER:
            d_out(yy).start()

    loads["u"].wait()
    u_own[...] = jnp.concatenate([u_v[0:1].astype(F32), u_v[1:2].astype(F32)], axis=1)

    @pl.when(half == 1)
    def _():
        for yy in Y_ORDER:
            u_out_over(yy).start()

    for name in ("x", "len", "bias", "q", "k", "v"):
        loads[name].start()
    for i in range(W_PARTS):
        w_load(i).start()

    span = NT * D_ROWS
    per = HEAD // D_ROWS
    groups = NQ // per
    shape = (per * span, HEAD)
    block = iota(shape, 1) // D_ROWS
    owner = jnp.where(lax.rem(block, 2) == half, t, mirror)
    pick = (iota(shape, 0) // span == block) & (
        lax.rem(iota(shape, 0), span) == owner * D_ROWS + lax.rem(iota(shape, 1), D_ROWS)
    )
    pick = jnp.where(pick, 1.0, 0.0).astype(BF16)
    loads["x"].wait()
    rows = []
    for j in range(NX):
        for g in range(groups):
            rows.append(
                jnp.concatenate(
                    [
                        stack_steps(x_v, pl.ds(((g * per + i) * NX + j) * span, span))
                        for i in range(per)
                    ],
                    axis=1,
                )
            )
    picked = dot(jnp.concatenate(rows, axis=0).astype(BF16), pick)
    for j in range(NX):
        for g in range(groups):
            base = (j * groups + g) * N
            for s in range(STEPS):
                xs[j, s, :, g * HEAD : (g + 1) * HEAD] = picked[
                    base + s * ROWS : base + (s + 1) * ROWS
                ].astype(BF16)
    xr[x] = xs[x]
    @pl.when(half == 0)
    def _():
        u_all[x, 0, y] = u_own[...]
        pl.semaphore_wait(barrier, NY + NX + NT - 3)
        for d in range(1, NY):
            d_out(plus(y, d, NY)).start()
        for d in range(1, NX):
            x_copy(d, x).start()
        for d in range(1, NY):
            u_out(plus(y, d, NY)).start()

    for name in ("q", "k", "len"):
        loads[name].wait()
    queries = jnp.concatenate(
        [
            q_v[s, :, h * HEAD : (h + 1) * HEAD].astype(F32)
            for s in range(STEPS)
            for h in range(GROUP)
        ],
        axis=0,
    ).astype(BF16)
    qb[...] = queries
    scale = HEAD**-0.5
    row = iota((ROWS, HEAD), 0)
    length = jnp.zeros((ROWS, HEAD), jnp.int32)
    for b in range(ROWS):
        length = jnp.where(row == b, len_s[b], length)
    column = iota((ROWS, SLOTS), 1)
    valid = (column // CACHE == iota((ROWS, SLOTS), 0)) & (
        lax.rem(column, CACHE) < jnp.concatenate([length] * (SLOTS // HEAD), axis=1)
    )
    scores = dot_t(queries, k_v[...].reshape(SLOTS, HEAD)) * scale
    scores = jnp.where(
        valid[None], scores.reshape(STEPS * GROUP, ROWS, SLOTS), MASKED
    ).reshape(M, SLOTS)
    peak = jnp.max(scores, axis=-1, keepdims=True)
    raised = jnp.exp(scores - peak)
    peak_c[...] = jnp.broadcast_to(peak, (M, HEAD))
    total_c[...] = jnp.broadcast_to(jnp.sum(raised, axis=-1, keepdims=True), (M, HEAD))
    loads["v"].wait()
    acc_c[...] = dot(raised.astype(BF16), v_v[...].reshape(SLOTS, HEAD))

    for s in range(STEPS):
        xb[pl.ds(s * ROWS, ROWS)] = x_v[s].astype(F32)
    proj[...] = jnp.zeros_like(proj)

    def project(i, carry):
        w_load(i).wait()
        rows = pl.ds(pl.multiple_of(i * part, part), part)
        proj[...] += dot(
            xb[:, rows].astype(BF16), jnp.concatenate([w_v[0, rows], w_v[1, rows]], axis=1)
        )
        return carry

    lax.fori_loop(0, W_PARTS, project, 0)

    loads["bias"].wait()
    proj[...] += jnp.concatenate([bias_v[0:1], bias_v[1:2]], axis=1).astype(F32)
    turn = HEAD // 2
    lane = iota((ROWS, HEAD), 1)
    frequency = jnp.exp(lax.rem(lane, turn).astype(F32) * (-2.0 / HEAD * math.log(ROPE_BASE)))
    for s in range(STEPS):
        angle = (length + s).astype(F32) * frequency
        cos_v[pl.ds(s * ROWS, ROWS)] = jnp.cos(angle)
        sine = jnp.sin(angle)
        sin_v[pl.ds(s * ROWS, ROWS)] = jnp.where(lane < turn, -sine, sine)

    def gather_x():
        x_all[...] = jnp.concatenate(
            [stack_steps(xr.at[j], slice(None)) for j in range(NX)], axis=0
        ).astype(BF16)

    @pl.when(half == 0)
    def _():
        d_load.wait()
        d_in(q + 1).wait_recv()
        for d in range(1, NX):
            signal(near_x, (at(y, 0, plus(x, d, NX)), t))
        for d in range(1, NT):
            signal(near_t, (f, plus(t, d, NT)))
        for d in range(1, NX):
            x_copy(d, from_x(d)).wait_recv()
        gather_x()
        for d in range(1, NY):
            d_in(plus(y, d, NY) * 2).wait_recv()
            d_in(plus(y, d, NY) * 2 + 1).wait_recv()

    @pl.when(half == 1)
    def _():
        pl.semaphore_wait(go_x, 1)
        for d in range(1, NX):
            x_copy(d, x).start()
        for d in range(1, NX):
            x_copy(d, from_x(d)).wait_recv()
        gather_x()
        d_over().wait_recv()

    partial = dot(x_all[...], d_all[...].reshape(NQ * D_ROWS, HEAD))
    for j in range(NX):
        for s in range(STEPS):
            base = j * N + s * ROWS
            pp[j, s] = partial[base : base + ROWS]
    for d in (2, 1, 3):
        p_copy(d, x).start()
    pr[x] = pp[x]

    @pl.when(half == 0)
    def _():
        d_over().start()
        pl.semaphore_wait(near_x, NX - 1)
        signal(go_x, (at(y, 1, x), mirror))
        for d in range(1, NY):
            u_in(plus(y, d, NY)).wait_recv()
        for d in range(1, NX):
            u2_half(d, x).start()
        for yy in range(NY):
            u_in_over(yy).wait_recv()
        for xx in range(NX):
            u_home(xx).start()

    @pl.when(half == 1)
    def _():
        for h in range(2):
            u_back(h).wait_recv()
        for d in range(1, NX):
            u2_both(d, x).start()

    for d in range(1, NX):
        p_copy(d, from_x(d)).wait_recv()
    for s in range(STEPS):
        pt[t, s] = pr[0, s] + pr[1, s] + pr[2, s] + pr[3, s]

    @pl.when(half == 1)
    def _():
        pl.semaphore_wait(go_t, 1)

    for to in T_ORDER:

        @pl.when(t != to)
        def _(to=to):
            t_out(to).start()

    @pl.when(half == 0)
    def _():
        pl.semaphore_wait(near_t, NT - 1)
        signal(go_t, (at(y, 1, x), mirror))
        for h in range(2):
            u_back(h).start()

    @pl.when(half == 0)
    def _():
        for d in range(1, NX):
            u2_half(d, from_x(d)).wait_recv()
        for xx in range(NX):
            u_home_in(xx).wait_recv()

    @pl.when(half == 1)
    def _():
        for d in range(1, NX):
            u2_both(d, from_x(d)).wait_recv()

    ranks = NQ * NX
    order = iota((ranks, ranks), 0)
    order = iota((ranks, ranks), 1) == (
        lax.rem(order, NX) * NQ + lax.rem(order // NX, 2) * NY + order // (2 * NX)
    )
    rows = u_all[...].reshape(ranks, 2 * HEAD).astype(BF16)
    up = dot(jnp.where(order, 1.0, 0.0).astype(BF16), rows)
    up = up * ADAPTER_SCALE
    which = iota((ranks, 2 * HEAD), 1) < HEAD
    ublk[...] = jnp.concatenate(
        [jnp.where(which, up, 0.0), jnp.where(which, 0.0, up)], axis=0
    ).astype(BF16)

    @pl.when(half == 0)
    def _():
        for d in range(1, NY):
            d_out(plus(y, d, NY)).wait_send()
            u_out(plus(y, d, NY)).wait_send()
        d_over().wait_send()
        for xx in range(NX):
            u_home(xx).wait_send()
        for h in range(2):
            u_back(h).wait_send()
        for d in range(1, NX):
            u2_half(d, x).wait_send()

    @pl.when(half == 1)
    def _():
        for yy in range(NY):
            d_out(yy).wait_send()
            u_out_over(yy).wait_send()
        for d in range(1, NX):
            u2_both(d, x).wait_send()

    for d in range(1, NX):
        x_copy(d, x).wait_send()
        p_copy(d, x).wait_send()

    for d in range(1, NT):
        t_in(from_t(d)).wait_recv()
    sums = []
    for s in range(STEPS):
        total = pt[0, s]
        for i in range(1, NT):
            total = total + pt[i, s]
        sums.append(total)
    low_rank = jnp.concatenate(sums, axis=0)
    high = low_rank.astype(BF16).astype(F32)
    both = jnp.concatenate([high, low_rank - high], axis=0).astype(BF16)
    change = dot(both, ublk[...])
    fresh = proj[...] + change[:N] + change[N:]
    key = fresh[:, :HEAD]
    key = key * cos_v[...] + pltpu.roll(key, turn, axis=1) * sin_v[...]
    value = fresh[:, HEAD:]
    for s in range(STEPS):
        ent_v[0, s] = key[s * ROWS : (s + 1) * ROWS].astype(BF16)
        ent_v[1, s] = value[s * ROWS : (s + 1) * ROWS].astype(BF16)
    scores = dot_t(qb[...], key.astype(BF16)) * scale
    r, c = iota((M, N), 0), iota((M, N), 1)
    scores = jnp.where(
        (lax.rem(r, ROWS) == lax.rem(c, ROWS)) & (c // ROWS <= r // (GROUP * ROWS)), scores, MASKED
    )
    peak_old = peak_c[:, 0:1]
    peak = jnp.maximum(peak_old, jnp.max(scores, axis=-1, keepdims=True))
    raised = jnp.exp(scores - peak)
    shrink = jnp.exp(peak_old - peak)
    total = shrink * total_c[:, 0:1] + jnp.sum(raised, axis=-1, keepdims=True)
    out = (shrink * acc_c[...] + dot(raised.astype(BF16), value.astype(BF16))) / total
    for s in range(STEPS):
        for h in range(GROUP):
            base = (s * GROUP + h) * ROWS
            att_v[s, :, h * HEAD : (h + 1) * HEAD] = out[base : base + ROWS].astype(BF16)

    for d in range(1, NT):
        t_out(from_t(d)).wait_send()


def deliver(att_v, ent_v, att_hbm, ent_hbm, sem):
    copies = [
        pltpu.make_async_copy(att_v, att_hbm, sem.at[0]),
        pltpu.make_async_copy(ent_v, ent_hbm, sem.at[1]),
    ]
    for copy in copies:
        copy.start()
    for copy in copies:
        copy.wait()


def body(x, lengths, queries, keys, values, weight, bias, down, up):
    width = x.shape[2]
    vmem = pltpu.VMEM
    dma = pltpu.SemaphoreType.DMA
    anywhere = pl.BlockSpec(memory_space=pl.ANY)
    inside = pl.BlockSpec(memory_space=pltpu.VMEM)
    entries = (2, STEPS, ROWS, HEAD)
    attended, entry = pl.pallas_call(
        kernel,
        out_shape=(pltpu.VMEM(queries.shape, BF16), pltpu.VMEM(entries, BF16)),
        in_specs=[anywhere] * 9,
        out_specs=(inside, inside),
        scratch_shapes=[
            vmem(x.shape, BF16),
            pltpu.SMEM(lengths.shape, jnp.int32),
            vmem(queries.shape, BF16),
            vmem(keys.shape, BF16),
            vmem(values.shape, BF16),
            vmem(weight.shape, BF16),
            vmem(bias.shape, BF16),
            vmem((2, HEAD), BF16),
            vmem((1, 2 * HEAD), F32),
            vmem((NQ, D_ROWS, HEAD), BF16),
            vmem((NX, STEPS, ROWS, NQ * D_ROWS), BF16),
            vmem((NX, STEPS, ROWS, NQ * D_ROWS), BF16),
            vmem((NX * N, NQ * D_ROWS), BF16),
            vmem((NX, 2, NY, 1, 2 * HEAD), F32),
            vmem((NY, 1, 2 * HEAD), F32),
            vmem((NX, STEPS, ROWS, HEAD), F32),
            vmem((NX, STEPS, ROWS, HEAD), F32),
            vmem((NT, STEPS, ROWS, HEAD), F32),
            vmem((N, width), F32),
            vmem((N, 2 * HEAD), F32),
            vmem((N, HEAD), F32),
            vmem((N, HEAD), F32),
            vmem((M, HEAD), BF16),
            vmem((M, HEAD), F32),
            vmem((M, HEAD), F32),
            vmem((M, HEAD), F32),
            vmem((2 * NQ * NX, 2 * HEAD), BF16),
            dma((8,)),
            dma((W_PARTS,)),
            dma((NY,)),
            dma((NQ,)),
            dma((2,)),
            dma((NX,)),
            dma((NX,)),
            dma((NY,)),
            dma((NY, 2)),
            dma((NX,)),
            dma((NX,)),
            dma((2,)),
            dma((2,)),
            dma((NX,)),
            dma((NX,)),
            dma((NX,)),
            dma((NX,)),
            dma((NT,)),
            dma((NT,)),
            pltpu.SemaphoreType.REGULAR,
            pltpu.SemaphoreType.REGULAR,
            pltpu.SemaphoreType.REGULAR,
            pltpu.SemaphoreType.REGULAR,
        ],
        compiler_params=pltpu.CompilerParams(
            collective_id=0, has_side_effects=True, vmem_limit_bytes=60 * 1024 * 1024
        ),
        name="adapter_attention",
    )(x, lengths, queries, keys, values, weight, bias, down, up.reshape(2, HEAD))
    return pl.pallas_call(
        deliver,
        out_shape=(
            jax.ShapeDtypeStruct(queries.shape, BF16),
            jax.ShapeDtypeStruct(entries, BF16),
        ),
        in_specs=[inside] * 2,
        out_specs=(anywhere, anywhere),
        scratch_shapes=[dma((2,))],
        compiler_params=pltpu.CompilerParams(vmem_limit_bytes=1024 * 1024),
        name="deliver",
    )(attended, entry)


def solution(mesh):
    placed = (
        P(None, "fsdp", None),
        P("fsdp"),
        P(None, "fsdp", "tp"),
        P("fsdp", None, "tp"),
        P("fsdp", None, "tp"),
        P(None, None, "tp"),
        P(None, "tp"),
        P(("fsdp", "tp"), None),
        P(None, "fsdp", "tp"),
    )
    return jax.shard_map(
        body,
        mesh=mesh,
        in_specs=placed,
        out_specs=(P(None, "fsdp", "tp"), P(None, None, "fsdp", "tp")),
        check_vma=False,
    )
```

```python
import math

import jax
import jax.numpy as jnp
from jax import lax
from jax.experimental import pallas as pl
from jax.experimental.pallas import tpu as pltpu
from jax.sharding import PartitionSpec as P

HEAD = 128
GROUP = 8
STEPS = 3
ROWS = 8
CACHE = 64
NX = 4
NY = 8
NQ = 16
NT = 8
D_ROWS = 16
ADAPTER_SCALE = 2.0
ROPE_BASE = 1000000.0
MASKED = -1e30
MESH = pl.DeviceIdType.MESH
F32 = jnp.float32
BF16 = jnp.bfloat16
N = STEPS * ROWS
M = STEPS * GROUP * ROWS
SLOTS = ROWS * CACHE
W_PARTS = 8
T_ORDER = (1, 0, 3, 2, 5, 4, 7, 6)
Y_ORDER = (0, 1, 2, 3, 7, 6, 5, 4)


def iota(shape, dim):
    return lax.broadcasted_iota(jnp.int32, shape, dim)


def dot(a, b):
    return jnp.dot(a, b, preferred_element_type=F32)


def dot_t(a, b):
    return lax.dot_general(a, b, (((1,), (1,)), ((), ())), preferred_element_type=F32)


def stack_steps(ref, columns):
    return jnp.concatenate([ref[s, :, columns].astype(F32) for s in range(STEPS)], axis=0)


def kernel(
    x_hbm,
    len_hbm,
    q_hbm,
    k_hbm,
    v_hbm,
    w_hbm,
    bias_hbm,
    d_hbm,
    u_hbm,
    att_v,
    ent_v,
    x_v,
    len_s,
    q_v,
    k_v,
    v_v,
    w_v,
    bias_v,
    u_v,
    u_own,
    d_all,
    xs,
    xr,
    x_all,
    u_all,
    u_far,
    pp,
    pr,
    pt,
    xb,
    proj,
    cos_v,
    sin_v,
    qb,
    peak_c,
    total_c,
    acc_c,
    ublk,
    in_sem,
    w_sem,
    d_send,
    d_recv,
    df_sem,
    x_send,
    x_recv,
    u1_send,
    u1_recv,
    uh_send,
    uh_recv,
    ub_send,
    ub_recv,
    u2_send,
    u2_recv,
    p_send,
    p_recv,
    t_send,
    t_recv,
    near_x,
    near_t,
    go_x,
    go_t,
):
    f = lax.axis_index("fsdp")
    t = lax.axis_index("tp")
    q, x = f // NX, lax.rem(f, NX)
    y, half = q // 2, lax.rem(q, 2)
    mirror = (NT // 2 - 1 - t // 2) * 2 + lax.rem(t, 2)
    width = x_v.shape[2]

    def at(yy, hh, xx):
        return (yy * 2 + hh) * NX + xx

    def plus(i, d, n):
        return lax.rem(i + d, n)

    def load(i, src, dst):
        return pltpu.make_async_copy(src, dst, in_sem.at[i])

    loads = {
        "u": load(0, u_hbm, u_v),
        "x": load(1, x_hbm, x_v),
        "len": load(2, len_hbm, len_s),
        "bias": load(3, bias_hbm, bias_v),
        "q": load(4, q_hbm, q_v),
        "k": load(5, k_hbm, k_v),
        "v": load(6, v_hbm, v_v),
    }
    d_load = pltpu.make_async_copy(d_hbm, d_all.at[q], in_sem.at[7])
    part = width // W_PARTS

    def w_load(i):
        rows = pl.ds(pl.multiple_of(i * part, part), part)
        return pltpu.make_async_copy(w_hbm.at[:, rows], w_v.at[:, rows], w_sem.at[i])

    def remote(src, dst, send, recv, where):
        return pltpu.make_async_remote_copy(
            src_ref=src, dst_ref=dst, send_sem=send, recv_sem=recv, device_id=where, device_id_type=MESH
        )

    def d_out(yy):
        where = (at(yy, 0, x), jnp.where(half == 0, t, mirror))
        return remote(d_hbm, d_all.at[q], d_send.at[yy], d_recv.at[q], where)

    def d_in(qq):
        return remote(d_hbm, d_all.at[qq], d_send.at[0], d_recv.at[qq], (f, t))

    def u_out(yy):
        where = (at(yy, 0, x), t)
        return remote(u_own, u_all.at[x, 0, y], u1_send.at[yy], u1_recv.at[y, 0], where)

    def u_out_over(yy):
        where = (at(yy, 0, x), mirror)
        return remote(u_own, u_far.at[y], u1_send.at[yy], u1_recv.at[y, 1], where)

    def u_in(yy):
        return remote(u_own, u_all.at[x, 0, yy], u1_send.at[0], u1_recv.at[yy, 0], (f, t))

    def u_in_over(yy):
        return remote(u_own, u_far.at[yy], u1_send.at[0], u1_recv.at[yy, 1], (f, t))

    def u_home(xx):
        where = (at(y, 0, xx), mirror)
        return remote(u_far, u_all.at[x, 1], uh_send.at[xx], uh_recv.at[x], where)

    def u_home_in(xx):
        return remote(u_far, u_all.at[xx, 1], uh_send.at[xx], uh_recv.at[xx], (f, t))

    def u_back(h):
        source, to = ((u_all.at[x, 0], t), (u_far, mirror))[h]
        return remote(source, u_all.at[x, h], ub_send.at[h], ub_recv.at[h], (at(y, 1, x), to))

    def d_over():
        return remote(d_all, d_all, df_sem.at[0], df_sem.at[1], (at(y, 1 - half, x), mirror))

    def along_x(src, dst, send, recv, d):
        return remote(src, dst, send.at[d], recv.at[d], (at(y, half, plus(x, d, NX)), t))

    def x_copy(d, block):
        return along_x(xs.at[plus(x, d, NX)], xr.at[block], x_send, x_recv, d)

    def p_copy(d, block):
        return along_x(pp.at[plus(x, d, NX)], pr.at[block], p_send, p_recv, d)

    def u2_half(d, block):
        return along_x(u_all.at[block, 0], u_all.at[block, 0], u2_send, u2_recv, d)

    def u2_both(d, block):
        return along_x(u_all.at[block], u_all.at[block], u2_send, u2_recv, d)

    def t_out(to):
        return remote(pt.at[t], pt.at[t], t_send.at[to], t_recv.at[t], (f, to))

    def t_in(by):
        return remote(pt.at[by], pt.at[by], t_send.at[by], t_recv.at[by], (f, by))

    def from_x(d):
        return plus(x, NX - d, NX)

    def from_t(d):
        return plus(t, NT - d, NT)

    loads["u"].start()

    barrier = pltpu.get_barrier_semaphore()

    def signal(semaphore, where):
        pl.semaphore_signal(semaphore, inc=1, device_id=where, device_id_type=MESH)

    @pl.when(half == 0)
    def _():
        d_load.start()
        for yy in Y_ORDER:
            signal(barrier, (at(yy, 1, x), mirror))
        for d in range(1, NY):
            signal(barrier, (at(plus(y, d, NY), 0, x), t))
        for d in range(1, NX):
            signal(barrier, (at(y, 0, plus(x, d, NX)), t))
        for d in range(1, NT):
            signal(barrier, (f, plus(t, d, NT)))

    @pl.when(half == 1)
    def _():
        pl.semaphore_wait(barrier, NY)
        for yy in Y_ORDER:
            d_out(yy).start()

    loads["u"].wait()
    u_own[...] = jnp.concatenate([u_v[0:1].astype(F32), u_v[1:2].astype(F32)], axis=1)

    @pl.when(half == 1)
    def _():
        for yy in Y_ORDER:
            u_out_over(yy).start()

    for name in ("x", "len", "bias", "q", "k", "v"):
        loads[name].start()
    for i in range(W_PARTS):
        w_load(i).start()

    span = NT * D_ROWS
    per = HEAD // D_ROWS
    groups = NQ // per
    shape = (per * span, HEAD)
    block = iota(shape, 1) // D_ROWS
    owner = jnp.where(lax.rem(block, 2) == half, t, mirror)
    pick = (iota(shape, 0) // span == block) & (
        lax.rem(iota(shape, 0), span) == owner * D_ROWS + lax.rem(iota(shape, 1), D_ROWS)
    )
    pick = jnp.where(pick, 1.0, 0.0).astype(BF16)
    loads["x"].wait()
    rows = []
    for j in range(NX):
        for g in range(groups):
            rows.append(
                jnp.concatenate(
                    [
                        stack_steps(x_v, pl.ds(((g * per + i) * NX + j) * span, span))
                        for i in range(per)
                    ],
                    axis=1,
                )
            )
    picked = dot(jnp.concatenate(rows, axis=0).astype(BF16), pick)
    for j in range(NX):
        for g in range(groups):
            base = (j * groups + g) * N
            for s in range(STEPS):
                xs[j, s, :, g * HEAD : (g + 1) * HEAD] = picked[
                    base + s * ROWS : base + (s + 1) * ROWS
                ].astype(BF16)
    xr[x] = xs[x]
    @pl.when(half == 0)
    def _():
        u_all[x, 0, y] = u_own[...]
        pl.semaphore_wait(barrier, NY + NX + NT - 3)
        for d in range(1, NY):
            d_out(plus(y, d, NY)).start()
        for d in range(1, NX):
            x_copy(d, x).start()
        for d in range(1, NY):
            u_out(plus(y, d, NY)).start()

    for name in ("q", "k", "len"):
        loads[name].wait()
    queries = jnp.concatenate(
        [
            q_v[s, :, h * HEAD : (h + 1) * HEAD].astype(F32)
            for s in range(STEPS)
            for h in range(GROUP)
        ],
        axis=0,
    ).astype(BF16)
    qb[...] = queries
    scale = HEAD**-0.5
    row = iota((ROWS, HEAD), 0)
    length = jnp.zeros((ROWS, HEAD), jnp.int32)
    for b in range(ROWS):
        length = jnp.where(row == b, len_s[b], length)
    column = iota((ROWS, SLOTS), 1)
    valid = (column // CACHE == iota((ROWS, SLOTS), 0)) & (
        lax.rem(column, CACHE) < jnp.concatenate([length] * (SLOTS // HEAD), axis=1)
    )
    scores = dot_t(queries, k_v[...].reshape(SLOTS, HEAD)) * scale
    scores = jnp.where(
        valid[None], scores.reshape(STEPS * GROUP, ROWS, SLOTS), MASKED
    ).reshape(M, SLOTS)
    peak = jnp.max(scores, axis=-1, keepdims=True)
    raised = jnp.exp(scores - peak)
    peak_c[...] = jnp.broadcast_to(peak, (M, HEAD))
    total_c[...] = jnp.broadcast_to(jnp.sum(raised, axis=-1, keepdims=True), (M, HEAD))
    loads["v"].wait()
    acc_c[...] = dot(raised.astype(BF16), v_v[...].reshape(SLOTS, HEAD))

    for s in range(STEPS):
        xb[pl.ds(s * ROWS, ROWS)] = x_v[s].astype(F32)
    proj[...] = jnp.zeros_like(proj)

    def project(i, carry):
        w_load(i).wait()
        rows = pl.ds(pl.multiple_of(i * part, part), part)
        proj[...] += dot(
            xb[:, rows].astype(BF16), jnp.concatenate([w_v[0, rows], w_v[1, rows]], axis=1)
        )
        return carry

    lax.fori_loop(0, W_PARTS, project, 0)

    loads["bias"].wait()
    proj[...] += jnp.concatenate([bias_v[0:1], bias_v[1:2]], axis=1).astype(F32)
    turn = HEAD // 2
    lane = iota((ROWS, HEAD), 1)
    frequency = jnp.exp(lax.rem(lane, turn).astype(F32) * (-2.0 / HEAD * math.log(ROPE_BASE)))
    for s in range(STEPS):
        angle = (length + s).astype(F32) * frequency
        cos_v[pl.ds(s * ROWS, ROWS)] = jnp.cos(angle)
        sine = jnp.sin(angle)
        sin_v[pl.ds(s * ROWS, ROWS)] = jnp.where(lane < turn, -sine, sine)

    def gather_x():
        x_all[...] = jnp.concatenate(
            [stack_steps(xr.at[j], slice(None)) for j in range(NX)], axis=0
        ).astype(BF16)

    @pl.when(half == 0)
    def _():
        d_load.wait()
        d_in(q + 1).wait_recv()
        for d in range(1, NX):
            signal(near_x, (at(y, 0, plus(x, d, NX)), t))
        for d in range(1, NT):
            signal(near_t, (f, plus(t, d, NT)))
        for d in range(1, NX):
            x_copy(d, from_x(d)).wait_recv()
        gather_x()
        for d in range(1, NY):
            d_in(plus(y, d, NY) * 2).wait_recv()
            d_in(plus(y, d, NY) * 2 + 1).wait_recv()

    @pl.when(half == 1)
    def _():
        pl.semaphore_wait(go_x, 1)
        for d in range(1, NX):
            x_copy(d, x).start()
        for d in range(1, NX):
            x_copy(d, from_x(d)).wait_recv()
        gather_x()
        d_over().wait_recv()

    partial = dot(x_all[...], d_all[...].reshape(NQ * D_ROWS, HEAD))
    for j in range(NX):
        for s in range(STEPS):
            base = j * N + s * ROWS
            pp[j, s] = partial[base : base + ROWS]
    for d in (2, 1, 3):
        p_copy(d, x).start()
    pr[x] = pp[x]

    @pl.when(half == 0)
    def _():
        d_over().start()
        pl.semaphore_wait(near_x, NX - 1)
        signal(go_x, (at(y, 1, x), mirror))
        for d in range(1, NY):
            u_in(plus(y, d, NY)).wait_recv()
        for d in range(1, NX):
            u2_half(d, x).start()
        for yy in range(NY):
            u_in_over(yy).wait_recv()
        for xx in range(NX):
            u_home(xx).start()

    @pl.when(half == 1)
    def _():
        for h in range(2):
            u_back(h).wait_recv()
        for d in range(1, NX):
            u2_both(d, x).start()

    for d in range(1, NX):
        p_copy(d, from_x(d)).wait_recv()
    for s in range(STEPS):
        pt[t, s] = (pr[0, s] + pr[1, s] + pr[2, s] + pr[3, s]).astype(BF16)

    @pl.when(half == 1)
    def _():
        pl.semaphore_wait(go_t, 1)

    for to in T_ORDER:

        @pl.when(t != to)
        def _(to=to):
            t_out(to).start()

    @pl.when(half == 0)
    def _():
        pl.semaphore_wait(near_t, NT - 1)
        signal(go_t, (at(y, 1, x), mirror))
        for h in range(2):
            u_back(h).start()

    @pl.when(half == 0)
    def _():
        for d in range(1, NX):
            u2_half(d, from_x(d)).wait_recv()
        for xx in range(NX):
            u_home_in(xx).wait_recv()

    @pl.when(half == 1)
    def _():
        for d in range(1, NX):
            u2_both(d, from_x(d)).wait_recv()

    ranks = NQ * NX
    order = iota((ranks, ranks), 0)
    order = iota((ranks, ranks), 1) == (
        lax.rem(order, NX) * NQ + lax.rem(order // NX, 2) * NY + order // (2 * NX)
    )
    rows = u_all[...].reshape(ranks, 2 * HEAD).astype(BF16)
    up = dot(jnp.where(order, 1.0, 0.0).astype(BF16), rows)
    up = up * ADAPTER_SCALE
    which = iota((ranks, 2 * HEAD), 1) < HEAD
    ublk[...] = jnp.concatenate(
        [jnp.where(which, up, 0.0), jnp.where(which, 0.0, up)], axis=0
    ).astype(BF16)

    @pl.when(half == 0)
    def _():
        for d in range(1, NY):
            d_out(plus(y, d, NY)).wait_send()
            u_out(plus(y, d, NY)).wait_send()
        d_over().wait_send()
        for xx in range(NX):
            u_home(xx).wait_send()
        for h in range(2):
            u_back(h).wait_send()
        for d in range(1, NX):
            u2_half(d, x).wait_send()

    @pl.when(half == 1)
    def _():
        for yy in range(NY):
            d_out(yy).wait_send()
            u_out_over(yy).wait_send()
        for d in range(1, NX):
            u2_both(d, x).wait_send()

    for d in range(1, NX):
        x_copy(d, x).wait_send()
        p_copy(d, x).wait_send()

    for d in range(1, NT):
        t_in(from_t(d)).wait_recv()
    sums = []
    for s in range(STEPS):
        total = pt[0, s].astype(F32)
        for i in range(1, NT):
            total = total + pt[i, s].astype(F32)
        sums.append(total)
    low_rank = jnp.concatenate(sums, axis=0)
    high = low_rank.astype(BF16).astype(F32)
    both = jnp.concatenate([high, low_rank - high], axis=0).astype(BF16)
    change = dot(both, ublk[...])
    fresh = proj[...] + change[:N] + change[N:]
    key = fresh[:, :HEAD]
    key = key * cos_v[...] + pltpu.roll(key, turn, axis=1) * sin_v[...]
    value = fresh[:, HEAD:]
    for s in range(STEPS):
        ent_v[0, s] = key[s * ROWS : (s + 1) * ROWS].astype(BF16)
        ent_v[1, s] = value[s * ROWS : (s + 1) * ROWS].astype(BF16)
    scores = dot_t(qb[...], key.astype(BF16)) * scale
    r, c = iota((M, N), 0), iota((M, N), 1)
    scores = jnp.where(
        (lax.rem(r, ROWS) == lax.rem(c, ROWS)) & (c // ROWS <= r // (GROUP * ROWS)), scores, MASKED
    )
    peak_old = peak_c[:, 0:1]
    peak = jnp.maximum(peak_old, jnp.max(scores, axis=-1, keepdims=True))
    raised = jnp.exp(scores - peak)
    shrink = jnp.exp(peak_old - peak)
    total = shrink * total_c[:, 0:1] + jnp.sum(raised, axis=-1, keepdims=True)
    out = (shrink * acc_c[...] + dot(raised.astype(BF16), value.astype(BF16))) / total
    for s in range(STEPS):
        for h in range(GROUP):
            base = (s * GROUP + h) * ROWS
            att_v[s, :, h * HEAD : (h + 1) * HEAD] = out[base : base + ROWS].astype(BF16)

    for d in range(1, NT):
        t_out(from_t(d)).wait_send()


def deliver(att_v, ent_v, att_hbm, ent_hbm, sem):
    copies = [
        pltpu.make_async_copy(att_v, att_hbm, sem.at[0]),
        pltpu.make_async_copy(ent_v, ent_hbm, sem.at[1]),
    ]
    for copy in copies:
        copy.start()
    for copy in copies:
        copy.wait()


def body(x, lengths, queries, keys, values, weight, bias, down, up):
    width = x.shape[2]
    vmem = pltpu.VMEM
    dma = pltpu.SemaphoreType.DMA
    anywhere = pl.BlockSpec(memory_space=pl.ANY)
    inside = pl.BlockSpec(memory_space=pltpu.VMEM)
    entries = (2, STEPS, ROWS, HEAD)
    attended, entry = pl.pallas_call(
        kernel,
        out_shape=(pltpu.VMEM(queries.shape, BF16), pltpu.VMEM(entries, BF16)),
        in_specs=[anywhere] * 9,
        out_specs=(inside, inside),
        scratch_shapes=[
            vmem(x.shape, BF16),
            pltpu.SMEM(lengths.shape, jnp.int32),
            vmem(queries.shape, BF16),
            vmem(keys.shape, BF16),
            vmem(values.shape, BF16),
            vmem(weight.shape, BF16),
            vmem(bias.shape, BF16),
            vmem((2, HEAD), BF16),
            vmem((1, 2 * HEAD), F32),
            vmem((NQ, D_ROWS, HEAD), BF16),
            vmem((NX, STEPS, ROWS, NQ * D_ROWS), BF16),
            vmem((NX, STEPS, ROWS, NQ * D_ROWS), BF16),
            vmem((NX * N, NQ * D_ROWS), BF16),
            vmem((NX, 2, NY, 1, 2 * HEAD), F32),
            vmem((NY, 1, 2 * HEAD), F32),
            vmem((NX, STEPS, ROWS, HEAD), F32),
            vmem((NX, STEPS, ROWS, HEAD), F32),
            vmem((NT, STEPS, ROWS, HEAD), BF16),
            vmem((N, width), F32),
            vmem((N, 2 * HEAD), F32),
            vmem((N, HEAD), F32),
            vmem((N, HEAD), F32),
            vmem((M, HEAD), BF16),
            vmem((M, HEAD), F32),
            vmem((M, HEAD), F32),
            vmem((M, HEAD), F32),
            vmem((2 * NQ * NX, 2 * HEAD), BF16),
            dma((8,)),
            dma((W_PARTS,)),
            dma((NY,)),
            dma((NQ,)),
            dma((2,)),
            dma((NX,)),
            dma((NX,)),
            dma((NY,)),
            dma((NY, 2)),
            dma((NX,)),
            dma((NX,)),
            dma((2,)),
            dma((2,)),
            dma((NX,)),
            dma((NX,)),
            dma((NX,)),
            dma((NX,)),
            dma((NT,)),
            dma((NT,)),
            pltpu.SemaphoreType.REGULAR,
            pltpu.SemaphoreType.REGULAR,
            pltpu.SemaphoreType.REGULAR,
            pltpu.SemaphoreType.REGULAR,
        ],
        compiler_params=pltpu.CompilerParams(
            collective_id=0, has_side_effects=True, vmem_limit_bytes=60 * 1024 * 1024
        ),
        name="adapter_attention",
    )(x, lengths, queries, keys, values, weight, bias, down, up.reshape(2, HEAD))
    return pl.pallas_call(
        deliver,
        out_shape=(
            jax.ShapeDtypeStruct(queries.shape, BF16),
            jax.ShapeDtypeStruct(entries, BF16),
        ),
        in_specs=[inside] * 2,
        out_specs=(anywhere, anywhere),
        scratch_shapes=[dma((2,))],
        compiler_params=pltpu.CompilerParams(vmem_limit_bytes=1024 * 1024),
        name="deliver",
    )(attended, entry)


def solution(mesh):
    placed = (
        P(None, "fsdp", None),
        P("fsdp"),
        P(None, "fsdp", "tp"),
        P("fsdp", None, "tp"),
        P("fsdp", None, "tp"),
        P(None, None, "tp"),
        P(None, "tp"),
        P(("fsdp", "tp"), None),
        P(None, "fsdp", "tp"),
    )
    return jax.shard_map(
        body,
        mesh=mesh,
        in_specs=placed,
        out_specs=(P(None, "fsdp", "tp"), P(None, None, "fsdp", "tp")),
        check_vma=False,
    )
```
